32 devices in a mesh: rep: 4 (over x, core), grp: 8 (over z, y).
Axes of the slice: x: 2, y: 2, z: 4, core: 2. Of those that a mesh axis runs over, the one named last changes fastest.
Arguments:
- tokens: bfloat16 [2, 4, 8, 128, 2048], P(None, None, 'grp', 'rep'), may hold values from -6 to 6
- cotangent: bfloat16 [2, 4, 1024, 2048], P(None, 'rep', 'grp'), may hold values from -6 to 6
- seq_lengths: int32 [2, 4], replicated, may hold values from 256 to 1024, as said below
- bin_order: int32 [2, 4], replicated, may hold values from 0 to 3, each once within a row
- norm_gain: bfloat16 [2048], P('grp'), may hold values from 0.5 to 1.5
- w_query: bfloat16 [2048, 2048], P('grp'), may hold values from -0.125 to 0.125
- w_key: bfloat16 [2048, 2048], P('grp'), may hold values from -0.125 to 0.125
- w_value: bfloat16 [2048, 3456], P('grp'), may hold values from -0.125 to 0.125
- w_gate: bfloat16 [2048, 3456], P('grp'), may hold values from -0.125 to 0.125
- w_out: bfloat16 [3456, 2048], P('grp'), may hold values from -0.109375 to 0.109375
- mlp_gain: bfloat16 [2048], P('grp'), may hold values from 0.5 to 1.5
- w_proj: bfloat16 [2048, 3456], P('grp'), may hold values from -0.125 to 0.125
- w_up: bfloat16 [2048, 3456], P('grp'), may hold values from -0.125 to 0.125
- w_down: bfloat16 [3456, 2048], P('grp'), may hold values from -0.109375 to 0.109375
Outputs:
- bin_out: bfloat16 [2, 4, 1024, 2048], P(None, 'rep', 'grp')
- token_grad: bfloat16 [2, 4, 8, 128, 2048], P(None, None, 'grp', 'rep')
- norm_gain_grad: float32 [2048], P('grp')
- query_grad: float32 [2048, 2048], P('grp')
- key_grad: float32 [2048, 2048], P('grp')
- value_grad: float32 [2048, 3456], P('grp')
- gate_grad: float32 [2048, 3456], P('grp')
- out_grad: float32 [3456, 2048], P('grp')
- mlp_gain_grad: float32 [2048], P('grp')
- proj_grad: float32 [2048, 3456], P('grp')
- up_grad: float32 [2048, 3456], P('grp')
- down_grad: float32 [3456, 2048], P('grp')
The draws below stay inside these ranges and needn't reach their ends.
Inputs may be any that keep to these rules, and one draw needn't show every extreme that they name: `seq_lengths`: in every micro-batch some sequence has exactly 1024 live tokens. `bin_order`: each row is a permutation of the 4 bins.
All inputs are finite; a program needn't handle non-finite values.
Results may differ from the reference program's by a relative error of at most 0.019.
Values may be sent and summed in bfloat16 or wider, within the bound.
No kernel may reach another device: no remote copies, remote signals or barrier semaphores. Data moves between devices by JAX's collectives and lax.ppermute only.
A program may use at most 640 MiB of HBM per device.

```python
import math
import jax
import jax.numpy as jnp
from jax import lax

D = 2048
HEADS = 8
KEY_DIM = 256
VAL_DIM = 432
FF = 3456
MB = 2
QK = 2048
VD = 3456
BIN = 1024
ROWS = 128
BLOCKS = 8
NSEQ = 4


def draw_seq_lengths(key, part):
    first_key, second_key = jax.random.split(jax.random.fold_in(key, 11))
    base_lengths = jax.random.randint(first_key, (MB, NSEQ), BIN // 4, BIN + 1)
    chosen = jax.random.randint(second_key, (MB,), 0, NSEQ)
    full_hit = jnp.arange(NSEQ)[None, :] == chosen[:, None]
    return jnp.where(full_hit, BIN, base_lengths).astype(jnp.int32)


def block_scale(rng, extent, cuts, low, high):
    def one(axis_at, blocks):
        steps = jax.random.uniform(jax.random.fold_in(jax.random.fold_in(rng, 6), axis_at), (blocks,), jnp.float32, low / len(cuts), high / len(cuts))
        return jnp.repeat(jnp.exp(steps), extent[axis_at] // blocks).reshape((-1,) + (1,) * (len(extent) - axis_at - 1))

    factor_of = one(*cuts[0])
    for cut in cuts[1:]:
        factor_of = factor_of * one(*cut)
    return factor_of


def noise(own_key, dims, deviation, limit, shards=(), held_as=jnp.bfloat16):
    values = jax.random.normal(own_key, dims, jnp.float32) * deviation
    if len(shards) > 0:
        values = block_scale(own_key, dims, shards, -0.22, 0.18) * values
    return jnp.clip(values, min=-limit, max=limit).astype(held_as)


def setup_inputs(seed: int = 0) -> dict:
    seeds = jax.random.split(jax.random.key(seed), 15)
    return {
        "tokens": noise(seeds[0], (MB, NSEQ, BLOCKS, ROWS, D), 1.0, 6.0, ((2, 8), (3, 4))),
        "cotangent": noise(seeds[1], (MB, NSEQ, BIN, D), 1.0, 6.0, ((1, 4), (2, 8))),
        "seq_lengths": draw_seq_lengths(jax.random.fold_in(seeds[14], 71), 0),
        "bin_order": jax.vmap(lambda own: jax.random.permutation(own, NSEQ))(jax.random.split(seeds[3], MB)).reshape((MB, NSEQ)).astype(jnp.int32),
        "norm_gain": jnp.clip(1.0 + 0.1 * jax.random.normal(seeds[4], (D,), jnp.float32), 0.5, 1.5).astype(jnp.bfloat16),
        "w_query": noise(seeds[5], (D, QK), D ** -0.5, 0.125, ((0, 8),)),
        "w_key": noise(seeds[6], (D, QK), D ** -0.5, 0.125, ((0, 8),)),
        "w_value": noise(seeds[7], (D, VD), D ** -0.5, 0.125, ((0, 8),)),
        "w_gate": noise(seeds[8], (D, VD), D ** -0.5, 0.125, ((0, 8),)),
        "w_out": noise(seeds[9], (VD, D), VD ** -0.5, 0.109375, ((0, 8),)),
        "mlp_gain": jnp.clip(1.0 + 0.1 * jax.random.normal(seeds[10], (D,), jnp.float32), 0.5, 1.5).astype(jnp.bfloat16),
        "w_proj": noise(seeds[11], (D, FF), D ** -0.5, 0.125, ((0, 8),)),
        "w_up": noise(seeds[12], (D, FF), D ** -0.5, 0.125, ((0, 8),)),
        "w_down": noise(seeds[13], (FF, D), FF ** -0.5, 0.109375, ((0, 8),)),
    }


EPS = 1e-06
GROUP_EPS = 1.0
HIGH = lax.Precision.HIGHEST

@jax.custom_vjp
def low(v):
    return lax.optimization_barrier(v.astype(jnp.bfloat16)).astype(jnp.float32)

@jax.custom_vjp
def low_back(v):
    return v

def low_keep(v):
    return (low(v), None)

def low_pass(kept, grad):
    return (grad,)

def back_keep(v):
    return (v, None)

def back_low(kept, grad):
    return (low(grad),)
low.defvjp(low_keep, low_pass)
low_back.defvjp(back_keep, back_low)

def norm_rows(values, gain_vec):
    return values * lax.rsqrt(lax.optimization_barrier(jnp.mean(values * values, axis=-1, keepdims=True)) + EPS) * gain_vec

def rotate(values, cosine, sine):
    half_size = values.shape[-1] // 2
    front_half = values[..., :half_size]
    back_half = values[..., half_size:]
    return jnp.concatenate([front_half * cosine - back_half * sine, back_half * cosine + front_half * sine], axis=-1)

def rotary_tables(positions, key_size):
    frequency = jnp.exp(-jnp.arange(key_size // 2, dtype=jnp.float32) * (2.0 / key_size) * math.log(10000.0))
    angles = positions[:, None] * frequency[None, :]
    return (jnp.cos(angles), jnp.sin(angles))

def decay_tables(head_count, row_count):
    head_ids = jnp.arange(head_count, dtype=jnp.float32)
    log_gamma = jnp.log(1.0 - jnp.exp2(-5.0 - head_ids))
    positions = jnp.arange(row_count, dtype=jnp.float32)
    lag_steps = positions[:, None] - positions[None, :]
    inner_decay = jnp.where(lag_steps[None] >= 0, jnp.exp(jnp.maximum(lag_steps, 0.0)[None] * log_gamma[:, None, None]), 0.0)
    query_decay = jnp.exp((positions[:, None] + 1.0) * log_gamma[None, :])
    key_decay = jnp.exp((row_count - 1.0 - positions[:, None]) * log_gamma[None, :])
    block_decay = jnp.exp(row_count * log_gamma)
    return (inner_decay, query_decay, key_decay, block_decay)

def mix_tail(retained, gate_pre):
    normed = retained * lax.rsqrt(lax.optimization_barrier(jnp.mean(retained * retained, axis=-1, keepdims=True)) + GROUP_EPS)
    return jax.nn.silu(gate_pre) * normed.reshape(gate_pre.shape)

def glu_act(proj_pre, up_pre):
    return jax.nn.gelu(proj_pre, approximate=True) * up_pre

def matmul_high(left, right):
    return jnp.dot(left, right, precision=HIGH)

def retention(query_rot, key_rot, value_rows):
    inner_decay, query_decay, key_decay, block_decay = decay_tables(HEADS, ROWS)

    def block_step(state, pieces):
        query_blk, key_blk, value_blk = pieces
        scores = low_back(jnp.einsum('ihd,jhd->hij', query_blk, key_blk, precision=HIGH))
        weights_blk = low(scores * inner_decay)
        intra = jnp.einsum('hij,jhe->ihe', weights_blk, value_blk, precision=HIGH)
        query_dec = low(query_blk * query_decay[:, :, None])
        cross = jnp.einsum('ihd,hde->ihe', query_dec, low(state), precision=HIGH)
        key_dec = low(key_blk * key_decay[:, :, None])
        local_state = low_back(jnp.einsum('jhd,jhe->hde', key_dec, value_blk, precision=HIGH))
        return (state * block_decay[:, None, None] + local_state, intra + cross)

    def split_blocks(array):
        return array.reshape(BLOCKS, ROWS, HEADS, array.shape[-1])
    start_state = jnp.zeros((HEADS, KEY_DIM, VAL_DIM), jnp.float32)
    final_state, retained = lax.scan(jax.checkpoint(block_step), start_state, (split_blocks(query_rot), split_blocks(key_rot), split_blocks(value_rows)))
    return retained.reshape(BIN, HEADS, VAL_DIM)

def layer(params, rows_in):
    gain_first, w_query, w_key, w_value, w_gate, w_out, gain_second, w_proj, w_up, w_down = params
    positions = jnp.arange(BIN, dtype=jnp.float32)
    cosine, sine = rotary_tables(positions, KEY_DIM)
    cosine_rows = cosine[:, None, :]
    sine_rows = sine[:, None, :]
    activations = low(norm_rows(rows_in, gain_first))
    query_pre = low_back(matmul_high(activations, w_query)).reshape(BIN, HEADS, KEY_DIM)
    key_pre = low_back(matmul_high(activations, w_key)).reshape(BIN, HEADS, KEY_DIM)
    value_rows = low(low_back(matmul_high(activations, w_value))).reshape(BIN, HEADS, VAL_DIM)
    gate_pre = low_back(matmul_high(activations, w_gate))
    query_rot = low(rotate(query_pre, cosine_rows, sine_rows))
    key_rot = low(rotate(key_pre, cosine_rows, sine_rows))
    retained = low_back(retention(query_rot, key_rot, value_rows))
    mixed = low(mix_tail(retained, gate_pre))
    hidden = rows_in + low_back(matmul_high(mixed, w_out))
    middle = low(norm_rows(hidden, gain_second))
    proj_pre = low_back(matmul_high(middle, w_proj))
    up_pre = low_back(matmul_high(middle, w_up))
    glu_rows = low(glu_act(proj_pre, up_pre))
    return hidden + low_back(matmul_high(glu_rows, w_down))

def reference(tokens, cotangent, seq_lengths, bin_order, norm_gain, w_query, w_key, w_value, w_gate, w_out, mlp_gain, w_proj, w_up, w_down):
    inverse = jnp.argsort(bin_order, axis=1).astype(jnp.int32)
    placed = jnp.take_along_axis(tokens, inverse[:, :, None, None, None], axis=1).reshape(MB * NSEQ, BIN, D).astype(jnp.float32)
    live_len = jnp.take_along_axis(seq_lengths, inverse, axis=1)
    live = (jnp.arange(BIN, dtype=jnp.int32)[None, None, :] < live_len[:, :, None]).astype(jnp.float32)
    cot_rows = (cotangent.astype(jnp.float32) * live[..., None]).reshape(MB * NSEQ, BIN, D)
    params = tuple((weight.astype(jnp.float32) for weight in (norm_gain, w_query, w_key, w_value, w_gate, w_out, mlp_gain, w_proj, w_up, w_down)))

    def one_sequence(totals, pieces):
        rows_in, cot_in = pieces
        result, pullback = jax.vjp(layer, params, rows_in)
        param_grads, input_grad = pullback(cot_in)
        totals = jax.tree.map(lambda left, right: left + right, totals, param_grads)
        return (totals, (result.astype(jnp.bfloat16), input_grad.astype(jnp.bfloat16)))
    zero_grads = jax.tree.map(jnp.zeros_like, params)
    totals, (results, input_grads) = lax.scan(one_sequence, zero_grads, (placed, cot_rows))
    bin_out = results.reshape(MB, NSEQ, BIN, D)
    back_rows = input_grads.reshape(MB, NSEQ, BLOCKS, ROWS, D)
    token_grad = jnp.take_along_axis(back_rows, bin_order[:, :, None, None, None], axis=1)
    return (bin_out, token_grad, totals[0], totals[1], totals[2], totals[3], totals[4], totals[5], totals[6], totals[7], totals[8], totals[9])
```

```python
import math

import jax
import jax.numpy as jnp
from jax import lax
from jax.sharding import PartitionSpec as P

HEADS = 8
KEY_DIM = 256
VAL_DIM = 432

EPS = 1e-06
GROUP_EPS = 1.0

f32 = jnp.float32
bf16 = jnp.bfloat16


def norm_rows(values, gain_vec):
    return values * lax.rsqrt(jnp.mean(values * values, axis=-1, keepdims=True) + EPS) * gain_vec


def dot(left, right):
    return jnp.dot(left, right, preferred_element_type=f32)


def dot_t(left, right):
    return lax.dot_general(left, right, (((1,), (1,)), ((), ())), preferred_element_type=f32)


def t_dot(left, right):
    return lax.dot_general(left, right, (((0,), (0,)), ((), ())), preferred_element_type=f32)


def swap(value, bit):
    count = lax.axis_size("rep")
    return lax.ppermute(value, "rep", [(i, i ^ bit) for i in range(count)])


def bits_high():
    count = lax.axis_size("rep")
    return [1 << b for b in reversed(range(count.bit_length() - 1))]


def pieces_of_replicas(value):
    pieces = {0: value}
    for bit in bits_high():
        for place in list(pieces):
            pieces[place | bit] = swap(pieces[place], bit)
    return [pieces[place] for place in range(len(pieces))]


def rows_of_replicas(value):
    return jnp.concatenate(pieces_of_replicas(value), axis=0)


def sum_to_replicas(partial):
    count = lax.axis_size("rep")
    rows = partial.shape[0] // count
    held = {o: partial[o * rows : (o + 1) * rows] for o in range(count)}
    for bit in reversed(bits_high()):
        places = [o for o in held if not o & bit]
        sent = jnp.concatenate([held[o | bit] for o in places], axis=0).astype(bf16)
        came = swap(sent, bit)
        held = {
            o: held[o].astype(f32) + came[i * rows : (i + 1) * rows].astype(f32)
            for i, o in enumerate(places)
        }
    return held[0]


def columns_of_replicas(value):
    count = lax.axis_size("rep")
    rank = lax.axis_index("rep")
    stacked = jnp.stack(pieces_of_replicas(value))
    return jnp.concatenate(
        [lax.dynamic_index_in_dim(stacked, rank ^ o, 0, False) for o in range(count)], axis=1
    )


def own_columns(weight):
    count = lax.axis_size("rep")
    width = weight.shape[1] // count
    return lax.dynamic_slice_in_dim(weight, lax.axis_index("rep") * width, width, 1)


def gather_members(part):
    return lax.all_gather(part, "grp", axis=0, tiled=True)


def scatter_members(full):
    return lax.psum_scatter(full, "grp", scatter_dimension=0, tiled=True)


def slab_route():
    reps, members = lax.axis_size("rep"), lax.axis_size("grp")
    per = members // reps
    return [
        (s * members + m, (m // per) * members + reps * (m % per) + s)
        for s in range(reps)
        for m in range(members)
    ]


def gather_slab(weight):
    reps, members = lax.axis_size("rep"), lax.axis_size("grp")
    per = members // reps
    piece = lax.ppermute(own_columns(weight), ("rep", "grp"), slab_route())
    rows, width = piece.shape
    full = gather_members(piece).reshape(per, reps, rows, width)
    return full.transpose(0, 2, 1, 3).reshape(per * rows, reps * width)


def scatter_slab(grad):
    reps, members = lax.axis_size("rep"), lax.axis_size("grp")
    per = members // reps
    rows, width = grad.shape[0] // per, grad.shape[1] // reps
    parts = grad.reshape(per, rows, reps, width).transpose(0, 2, 1, 3)
    owned = scatter_members(parts.reshape(members * rows, width))
    piece = lax.ppermute(owned, ("rep", "grp"), [(b, a) for a, b in slab_route()])
    return columns_of_replicas(piece).astype(f32)


def body(
    tokens,
    cotangent,
    seq_lengths,
    bin_order,
    norm_gain,
    w_query,
    w_key,
    w_value,
    w_gate,
    w_out,
    mlp_gain,
    w_proj,
    w_up,
    w_down,
):
    reps, members = lax.axis_size("rep"), lax.axis_size("grp")
    rank, member = lax.axis_index("rep"), lax.axis_index("grp")
    micro, seqs, _, strip, width = tokens.shape
    own_rows = members * strip
    block = reps * strip
    heads = HEADS // reps
    qk_cols = heads * KEY_DIM
    val_cols = heads * VAL_DIM

    x_b = lax.all_to_all(
        tokens.reshape(members, strip, width), "grp", split_axis=0, concat_axis=0, tiled=True
    ).reshape(own_rows, width)
    x = x_b.astype(f32)

    gains = lax.all_gather(jnp.stack([norm_gain, mlp_gain]), "grp", axis=1, tiled=True).astype(f32)
    gain_one, gain_two = gains[0], gains[1]

    weight_qk = gather_members(jnp.concatenate([own_columns(w_query), own_columns(w_key)], axis=1))
    weight_vg = gather_members(jnp.concatenate([own_columns(w_value), own_columns(w_gate)], axis=1))
    weight_out = gather_slab(w_out)
    weight_pu = gather_members(jnp.concatenate([own_columns(w_proj), own_columns(w_up)], axis=1))
    weight_down = gather_slab(w_down)
    hid_cols = weight_down.shape[0]

    selector = (
        bin_order[:, :, None] == jnp.arange(seqs, dtype=jnp.int32)[None, None, :]
    ).astype(bf16)
    cot_bins = lax.all_to_all(
        cotangent.reshape(micro, reps, strip, width), "rep", split_axis=1, concat_axis=1, tiled=True
    )
    cot_seqs = jnp.einsum("msk,mkrd->msrd", selector, cot_bins, preferred_element_type=f32)
    cot_own = lax.all_to_all(
        cot_seqs.astype(bf16).reshape(members, strip, width),
        "grp",
        split_axis=0,
        concat_axis=0,
        tiled=True,
    ).reshape(own_rows, width)

    strip_pos = (
        jnp.arange(members, dtype=jnp.int32)[:, None] * block
        + jnp.arange(strip, dtype=jnp.int32)[None, :]
    ).reshape(own_rows)
    positions = jnp.concatenate([strip_pos + strip * (rank ^ o) for o in range(reps)])
    live_len = lax.dynamic_index_in_dim(seq_lengths.reshape(-1), member, 0, False)
    live = (positions[:own_rows] < live_len).astype(f32)[:, None]
    out_grad = cot_own.astype(f32) * live
    out_grad_full = rows_of_replicas(out_grad.astype(bf16))

    normed, norm_pullback = jax.vjp(norm_rows, x, gain_one)
    acts = rows_of_replicas(normed.astype(bf16))
    qk_pre = dot(acts, weight_qk)
    vg_pre = dot(acts, weight_vg)
    value = vg_pre[:, :val_cols].astype(bf16)
    gate_pre = vg_pre[:, val_cols:]

    frequency = jnp.exp(
        -jnp.arange(KEY_DIM // 2, dtype=f32) * (2.0 / KEY_DIM) * math.log(10000.0)
    )
    angles = positions.astype(f32)[:, None] * frequency[None, :]
    cosine, sine = jnp.cos(angles), jnp.sin(angles)

    def turn(pre, sign):
        half = KEY_DIM // 2
        front, back = pre[:, :half], pre[:, half:]
        return jnp.concatenate(
            [front * cosine - sign * back * sine, back * cosine + sign * front * sine], axis=1
        )

    lag = (positions[:, None] - positions[None, :]).astype(f32)

    def decay(h):
        head = (rank * heads + h).astype(f32)
        log_gamma = jnp.log(1.0 - jnp.exp2(-5.0 - head))
        return jnp.where(lag >= 0, jnp.exp(jnp.maximum(lag, 0.0) * log_gamma), 0.0)

    def mix_tail(retained, gate):
        normed = retained * lax.rsqrt(
            jnp.mean(retained * retained, axis=-1, keepdims=True) + GROUP_EPS
        )
        return jax.nn.silu(gate) * normed

    query, key, values, weights, mixed, tails = [], [], [], [], [], []
    for h in range(heads):
        query.append(turn(qk_pre[:, h * KEY_DIM : (h + 1) * KEY_DIM], 1.0).astype(bf16))
        key.append(
            turn(qk_pre[:, qk_cols + h * KEY_DIM : qk_cols + (h + 1) * KEY_DIM], 1.0).astype(bf16)
        )
        values.append(value[:, h * VAL_DIM : (h + 1) * VAL_DIM])
        weights.append((dot_t(query[h], key[h]) * decay(h)).astype(bf16))
        retained = dot(weights[h], values[h])
        mix, pull = jax.vjp(mix_tail, retained, gate_pre[:, h * VAL_DIM : (h + 1) * VAL_DIM])
        mixed.append(mix.astype(bf16))
        tails.append(pull)
    mixed_b = jnp.concatenate(mixed, axis=1)

    hidden = x + sum_to_replicas(dot(mixed_b, weight_out))
    normed_mid, mid_pullback = jax.vjp(norm_rows, hidden, gain_two)
    middle = rows_of_replicas(normed_mid.astype(bf16))
    pu_pre = dot(middle, weight_pu)

    def glu_act(proj_pre, up_pre):
        return jax.nn.gelu(proj_pre, approximate=True) * up_pre

    glu_rows, glu_pullback = jax.vjp(glu_act, pu_pre[:, :hid_cols], pu_pre[:, hid_cols:])
    glu_b = glu_rows.astype(bf16)
    out_rows = hidden + sum_to_replicas(dot(glu_b, weight_down))

    out_seqs = lax.all_to_all(
        out_rows.astype(bf16).reshape(members, strip, width),
        "grp",
        split_axis=0,
        concat_axis=0,
        tiled=True,
    ).reshape(micro, seqs, strip, width)
    out_bins = jnp.einsum("msk,msrd->mkrd", selector, out_seqs, preferred_element_type=f32)
    bin_out = lax.all_to_all(
        out_bins.astype(bf16), "rep", split_axis=1, concat_axis=1, tiled=True
    ).reshape(micro, 1, block, width)

    glu_grad = dot_t(out_grad_full, weight_down)
    proj_grad, up_grad = glu_pullback(glu_grad)
    pu_grad = jnp.concatenate([proj_grad, up_grad], axis=1).astype(bf16)
    down_owned = scatter_slab(t_dot(glu_b, out_grad_full).astype(bf16))
    pu_owned = scatter_members(t_dot(middle, pu_grad).astype(bf16))
    middle_grad = sum_to_replicas(dot_t(pu_grad, weight_pu))
    hidden_grad = out_grad + mid_pullback(middle_grad)[0]
    branch = rows_of_replicas(hidden_grad.astype(bf16))
    out_owned = scatter_slab(t_dot(mixed_b, branch).astype(bf16))
    mixed_grad = dot_t(branch, weight_out)

    query_grads, key_grads, value_grads, gate_grads = [], [], [], []
    for h in range(heads):
        retained_grad, gate_grad = tails[h](mixed_grad[:, h * VAL_DIM : (h + 1) * VAL_DIM])
        retained_b = retained_grad.astype(bf16)
        gate_grads.append(gate_grad.astype(bf16))
        score_b = (dot_t(retained_b, values[h]) * decay(h)).astype(bf16)
        value_grads.append(t_dot(weights[h], retained_b).astype(bf16))
        query_grads.append(turn(dot(score_b, key[h]), -1.0).astype(bf16))
        key_grads.append(turn(t_dot(score_b, query[h]), -1.0).astype(bf16))
    vg_grad = jnp.concatenate(value_grads + gate_grads, axis=1)
    qk_grad = jnp.concatenate(query_grads + key_grads, axis=1)
    vg_owned = scatter_members(t_dot(acts, vg_grad).astype(bf16))
    qk_owned = scatter_members(t_dot(acts, qk_grad).astype(bf16))
    act_grad = sum_to_replicas(dot_t(qk_grad, weight_qk) + dot_t(vg_grad, weight_vg))
    input_grad = hidden_grad + norm_pullback(act_grad)[0]
    token_grad = lax.all_to_all(
        input_grad.astype(bf16).reshape(members, strip, width),
        "grp",
        split_axis=0,
        concat_axis=0,
        tiled=True,
    ).reshape(tokens.shape)

    def finish(owned, split):
        return (
            columns_of_replicas(owned[:, :split]).astype(f32),
            columns_of_replicas(owned[:, split:]).astype(f32),
        )

    proj_owned, up_owned = finish(pu_owned, hid_cols)
    value_owned, gate_owned = finish(vg_owned, val_cols)
    query_owned, key_owned = finish(qk_owned, qk_cols)

    def gain_grad(gain, pairs):
        total = sum(jnp.sum(w.astype(f32) * g, axis=1) for w, g in pairs)
        return total / gain.astype(f32)

    gain_one_owned = gain_grad(
        norm_gain,
        (
            (w_query, query_owned),
            (w_key, key_owned),
            (w_value, value_owned),
            (w_gate, gate_owned),
        ),
    )
    gain_two_owned = gain_grad(mlp_gain, ((w_proj, proj_owned), (w_up, up_owned)))
    return (
        bin_out,
        token_grad,
        gain_one_owned,
        query_owned,
        key_owned,
        value_owned,
        gate_owned,
        out_owned,
        gain_two_owned,
        proj_owned,
        up_owned,
        down_owned,
    )


def solution(mesh):
    return jax.shard_map(
        body,
        mesh=mesh,
        in_specs=(
            P(None, None, "grp", "rep", None),
            P(None, "rep", "grp", None),
            P(),
            P(),
            P("grp"),
            P("grp", None),
            P("grp", None),
            P("grp", None),
            P("grp", None),
            P("grp", None),
            P("grp"),
            P("grp", None),
            P("grp", None),
            P("grp", None),
        ),
        out_specs=(
            P(None, "rep", "grp", None),
            P(None, None, "grp", "rep", None),
            P("grp"),
            P("grp", None),
            P("grp", None),
            P("grp", None),
            P("grp", None),
            P("grp", None),
            P("grp"),
            P("grp", None),
            P("grp", None),
            P("grp", None),
        ),
        check_vma=False,
    )
```

```python
import functools
import math

import jax
import jax.numpy as jnp
from jax import lax
from jax.experimental import pallas as pl
from jax.experimental.pallas import tpu as pltpu
from jax.sharding import PartitionSpec as P

HEADS = 8
KEY_DIM = 256
VAL_DIM = 432

EPS = 1e-06
GROUP_EPS = 1.0

f32 = jnp.float32
bf16 = jnp.bfloat16


def norm_rows(values, gain_vec):
    return values * lax.rsqrt(jnp.mean(values * values, axis=-1, keepdims=True) + EPS) * gain_vec


def dot(left, right):
    return jnp.dot(left, right, preferred_element_type=f32)


def dot_t(left, right):
    return lax.dot_general(left, right, (((1,), (1,)), ((), ())), preferred_element_type=f32)


def t_dot(left, right):
    return lax.dot_general(left, right, (((0,), (0,)), ((), ())), preferred_element_type=f32)


def swap(value, bit):
    count = lax.axis_size("rep")
    return lax.ppermute(value, "rep", [(i, i ^ bit) for i in range(count)])


def bits_high():
    count = lax.axis_size("rep")
    return [1 << b for b in reversed(range(count.bit_length() - 1))]


latest = {}


def fence(*states, rings=()):
    leaves, tree = jax.tree.flatten(states)
    marks = [mark for ring in rings for mark in ring.marks()]
    fenced = lax.optimization_barrier((leaves, marks))[0]
    latest["mark"] = min(fenced, key=lambda leaf: leaf.size)
    for state, new in zip(states, jax.tree.unflatten(tree, fenced)):
        state.update(new)


def pieces_far(value):
    pieces = {0: value}
    for bit in bits_high()[:-1]:
        for place in list(pieces):
            pieces[place | bit] = swap(pieces[place], bit)
    return pieces


def pieces_near(pieces):
    pieces = dict(pieces)
    for place in list(pieces):
        pieces[place | 1] = swap(pieces[place], 1)
    return [pieces[place] for place in range(len(pieces))]


def pieces_of_replicas(value):
    return pieces_near(pieces_far(value))


def rows_near(pieces):
    return jnp.concatenate(pieces_near(pieces), axis=0)


def sum_send(held, bit):
    places = [o for o in held if not o & bit]
    sent = jnp.concatenate([held[o | bit].astype(bf16) for o in places], axis=0)
    return swap(sent, bit)


def sum_take(held, came, bit):
    places = [o for o in held if not o & bit]
    rows = came.shape[0] // len(places)
    return {
        o: held[o].astype(f32) + came[i * rows : (i + 1) * rows].astype(f32)
        for i, o in enumerate(places)
    }


def by_place(partial):
    count = lax.axis_size("rep")
    rows = partial.shape[0] // count
    return {o: partial[o * rows : (o + 1) * rows] for o in range(count)}


def sum_far(held):
    for bit in reversed(bits_high()[:-1]):
        held = sum_take(held, sum_send(held, bit), bit)
    return held[0]


def own_columns(weight):
    count = lax.axis_size("rep")
    width = weight.shape[1] // count
    return lax.dynamic_slice_in_dim(weight, lax.axis_index("rep") * width, width, 1)


def ring_members():
    count = lax.axis_size("grp")
    return list(range(0, count, 2)) + list(range(count - 1, 0, -2))


def ring_place():
    count, member = lax.axis_size("grp"), lax.axis_index("grp")
    return jnp.where(member % 2 == 0, member // 2, count - (member + 1) // 2)


def ring_step(value, ahead):
    ring = ring_members()
    count = len(ring)
    return lax.ppermute(
        value, "grp", [(ring[i], ring[(i + ahead) % count]) for i in range(count)]
    )


def ring_member(ahead):
    count = lax.axis_size("grp")
    place = (ring_place() + ahead) % count
    return jnp.where(place < count // 2, 2 * place, 2 * (count - place) - 1)


def gather_members(part):
    return lax.all_gather(part, "grp", axis=0, tiled=True)


def scatter_members(full):
    return lax.psum_scatter(full, "grp", scatter_dimension=0, tiled=True)


class Ring:
    def __init__(self, wide):
        half = lax.axis_size("grp") // 2
        self.left = [half if way == wide else half - 1 for way in (0, 1)]
        self.came = [[], []]

    def rest(self):
        while max(self.left) > 0:
            self.tick(free=True)

    def marks(self):
        return [came[-2] for came in self.came if len(came) > 1]

    def tick(self, free=False):
        for way, ahead in enumerate((1, -1)):
            if self.left[way] > 0:
                value = self.next(way, ahead)
                if not free:
                    value = lax.optimization_barrier((value, latest["mark"]))[0]
                self.came[way].append(ring_step(value, ahead))
                self.left[way] -= 1


class Gather(Ring):
    def __init__(self, part, wide):
        super().__init__(wide)
        self.part = part

    def next(self, way, ahead):
        return self.came[way][-1] if self.came[way] else self.part

    def pieces(self):
        self.rest()
        count = lax.axis_size("grp")
        pieces = {0: self.part}
        for way, ahead in enumerate((1, -1)):
            for i, came in enumerate(self.came[way]):
                pieces[-ahead * (i + 1) % count] = came
        return [pieces[i] for i in range(count)]


class Scatter(Ring):
    def __init__(self, rows, grad, wide):
        super().__init__(wide)
        self.full = t_dot(rows, grad).astype(bf16)

    def term(self, i):
        size = self.full.shape[0] // lax.axis_size("grp")
        return lax.dynamic_slice_in_dim(self.full, ring_member(i) * size, size, 0)

    def next(self, way, ahead):
        term = self.term((ahead * self.left[way]) % lax.axis_size("grp"))
        if self.came[way]:
            term = term.astype(f32) + self.came[way][-1].astype(f32)
        return term.astype(bf16)

    def whole(self):
        self.rest()
        total = self.term(0).astype(f32)
        for came in self.came:
            total = total + came[-1].astype(f32)
        return total.astype(bf16)


def assemble_kernel(spots, order_ref, *refs):
    count = len(spots)
    pieces, full_ref, held, in_sems, out_sems = (
        refs[:count],
        refs[count],
        refs[count + 1 : 2 * count + 1],
        refs[2 * count + 1],
        refs[2 * count + 2],
    )
    comes, goes = [], []
    for i, (place, member_rows, row, column) in enumerate(spots):
        rows, columns = pieces[i].shape
        start = pl.multiple_of(order_ref[place] * member_rows + row, rows)
        spot = full_ref.at[pl.ds(start, rows), pl.ds(column, columns)]
        comes.append(pltpu.make_async_copy(pieces[i], held[i], in_sems.at[i]))
        goes.append(pltpu.make_async_copy(held[i], spot, out_sems.at[i]))
    for come in comes:
        come.start()
    for come, go in zip(comes, goes):
        come.wait()
        go.start()
    for go in goes:
        go.wait()


def assembled(streams, member_rows, columns):
    members = lax.axis_size("grp")
    order = jnp.stack([ring_member(i) for i in range(members)]).astype(jnp.int32)
    pieces, spots = [], []
    for gather, row, column in streams:
        for i, piece in enumerate(gather.pieces()):
            pieces.append(piece)
            spots.append((i, member_rows, row, column))
    dtype = pieces[0].dtype
    size = members * member_rows * columns * dtype.itemsize
    return pl.pallas_call(
        functools.partial(assemble_kernel, spots),
        out_shape=jax.ShapeDtypeStruct((members * member_rows, columns), dtype),
        in_specs=[pl.BlockSpec(memory_space=pltpu.SMEM)]
        + [pl.BlockSpec(memory_space=pl.ANY)] * len(pieces),
        out_specs=pl.BlockSpec(memory_space=pl.ANY),
        scratch_shapes=[pltpu.VMEM(piece.shape, dtype) for piece in pieces]
        + [pltpu.SemaphoreType.DMA((len(pieces),))] * 2,
        compiler_params=pltpu.CompilerParams(vmem_limit_bytes=size + (2 << 20)),
        cost_estimate=pl.CostEstimate(flops=0, bytes_accessed=2 * size, transcendentals=0),
    )(order, *pieces)


def finish_kernel(reps, spots, summed, rank_ref, *refs):
    count = len(spots)
    pieces, refs = refs[:reps], refs[reps:]
    if summed:
        gain_ref, refs = refs[0], refs[1:]
        weights, refs = refs[:count], refs[count:]
    outs, refs = refs[:count], refs[count:]

    def lay(rank):
        for out_ref, (column, width) in zip(outs, spots):
            for r in range(reps):
                piece = pieces[rank ^ r][:, column : column + width].astype(f32)
                out_ref[:, r * width : (r + 1) * width] = piece

    for rank in range(reps):
        pl.when(rank_ref[0] == rank)(functools.partial(lay, rank))
    if summed:
        total = 0.0
        for out_ref, weight in zip(outs, weights):
            grad = out_ref[...]
            total += jnp.sum(weight[...].astype(f32) * grad, axis=1, keepdims=True)
        refs[0][...] = total / gain_ref[...].astype(f32)


def finished(pieces, spots, gain=None, weights=()):
    reps = len(pieces)
    rows, columns = pieces[0].shape
    step = rows
    for candidate in (64, 48, 72, 32):
        if rows % candidate == 0:
            step = candidate
            break
    rank = lax.axis_index("rep").astype(jnp.int32).reshape(1)

    def blocked(width):
        return pl.BlockSpec((step, width), lambda i: (i, 0))

    operands = [rank, *pieces]
    in_specs = [pl.BlockSpec(memory_space=pltpu.SMEM)] + [blocked(columns)] * reps
    shapes = [jax.ShapeDtypeStruct((rows, reps * width), f32) for _, width in spots]
    out_specs = [blocked(reps * width) for _, width in spots]
    if gain is not None:
        operands += [gain[:, None], *weights]
        in_specs += [blocked(1)] + [blocked(weight.shape[1]) for weight in weights]
        shapes.append(jax.ShapeDtypeStruct((rows, 1), f32))
        out_specs.append(blocked(1))
    size = sum(reps * width for _, width in spots) * rows
    return pl.pallas_call(
        functools.partial(finish_kernel, reps, spots, gain is not None),
        grid=(rows // step,),
        in_specs=in_specs,
        out_specs=out_specs,
        out_shape=shapes,
        compiler_params=pltpu.CompilerParams(vmem_limit_bytes=40 << 20),
        cost_estimate=pl.CostEstimate(flops=4 * size, bytes_accessed=8 * size, transcendentals=0),
    )(*operands)


def slab_routes():
    reps, members = lax.axis_size("rep"), lax.axis_size("grp")
    per = members // reps
    return [
        [
            (s * members + m, (m // per) * members + per * s + (m % per + turn) % per)
            for s in range(reps)
            for m in range(members)
        ]
        for turn in range(per)
    ]


def selected(choices, which):
    result = choices[0]
    for s in range(1, len(choices)):
        result = jnp.where(which == s, choices[s], result)
    return result


def slab_parts(weight):
    reps, members = lax.axis_size("rep"), lax.axis_size("grp")
    rank, member = lax.axis_index("rep"), lax.axis_index("grp")
    per = members // reps
    size = weight.shape[1] // members
    blocks = [per * rank + (member % per + turn) % per for turn in range(per)]
    return [lax.dynamic_slice_in_dim(weight, block * size, size, 1).T for block in blocks]


def slab_piece(parts):
    reps, members = lax.axis_size("rep"), lax.axis_size("grp")
    member = lax.axis_index("grp")
    per = members // reps
    came = [
        lax.ppermute(sent, ("rep", "grp"), route) for sent, route in zip(parts, slab_routes())
    ]
    return jnp.concatenate(
        [selected([came[(e - a) % per] for e in range(per)], member % per) for a in range(per)],
        axis=1,
    )


def slab_rows(owned):
    reps, members = lax.axis_size("rep"), lax.axis_size("grp")
    member = lax.axis_index("grp")
    per = members // reps
    rows = owned.shape[1] // per
    came = []
    for turn, route in enumerate(slab_routes()):
        owner = (member % per - turn + per) % per
        sent = lax.dynamic_slice_in_dim(owned, owner * rows, rows, 1)
        came.append(lax.ppermute(sent, ("rep", "grp"), [(b, a) for a, b in route]))
    mine = jnp.concatenate(
        [
            selected([came[(k - e) % per] for e in range(per)], member % per).T
            for k in range(per)
        ],
        axis=1,
    )
    return mine


def padded(value):
    gap = -value.shape[1] % 128
    return jnp.pad(value, ((0, 0), (0, gap))) if gap else value


def body(
    tokens,
    cotangent,
    seq_lengths,
    bin_order,
    norm_gain,
    w_query,
    w_key,
    w_value,
    w_gate,
    w_out,
    mlp_gain,
    w_proj,
    w_up,
    w_down,
):
    reps, members = lax.axis_size("rep"), lax.axis_size("grp")
    rank, member = lax.axis_index("rep"), lax.axis_index("grp")
    micro, seqs, _, strip, width = tokens.shape
    own_rows = members * strip
    block = reps * strip
    heads = HEADS // reps
    qk_cols = heads * KEY_DIM
    val_cols = heads * VAL_DIM
    hid_cols = w_proj.shape[1] // reps
    member_rows = width // members

    strip_pos = (
        jnp.arange(members, dtype=jnp.int32)[:, None] * block
        + jnp.arange(strip, dtype=jnp.int32)[None, :]
    ).reshape(own_rows)
    positions = jnp.concatenate([strip_pos + strip * (rank ^ o) for o in range(reps)])
    live_len = lax.dynamic_index_in_dim(seq_lengths.reshape(-1), member, 0, False)
    live = (positions[:own_rows] < live_len).astype(f32)[:, None]
    selector = (
        bin_order[:, :, None] == jnp.arange(seqs, dtype=jnp.int32)[None, None, :]
    ).astype(bf16)

    qkvg_own = jnp.concatenate(
        [padded(own_columns(weight)) for weight in (w_query, w_key, w_value, w_gate)],
        axis=1,
    )
    qkvg_cols = qkvg_own.shape[1]
    cut = qkvg_cols // 2
    qkvg = [Gather(qkvg_own[:, :cut], 0), Gather(qkvg_own[:, cut:], 1)]

    def tick(rings, free=False):
        for ring in rings:
            ring.tick(free)

    def mix_tail(retained, gate):
        normed = retained * lax.rsqrt(
            jnp.mean(retained * retained, axis=-1, keepdims=True) + GROUP_EPS
        )
        return jax.nn.silu(gate) * normed

    frequency = jnp.exp(
        -jnp.arange(KEY_DIM // 2, dtype=f32) * (2.0 / KEY_DIM) * math.log(10000.0)
    )
    angles = positions.astype(f32)[:, None] * frequency[None, :]
    log_gamma = jnp.log(1.0 - jnp.exp2(-5.0 - (rank * heads + jnp.arange(heads)).astype(f32)))
    spans = positions.astype(f32)[None, :] * log_gamma[:, None]
    t = {
        "cos": jnp.cos(angles),
        "sin": jnp.sin(angles),
        "grow": jnp.exp(spans),
        "shrink": jnp.exp(-spans),
    }

    for _ in range(members // 2):
        tick(qkvg, free=True)
    e = {
        "rows": lax.all_to_all(
            tokens.reshape(members, strip, width), "grp", split_axis=0, concat_axis=0, tiled=True
        ),
        "out": slab_parts(w_out),
        "down": slab_parts(w_down),
        "pu": [padded(own_columns(w_proj)), padded(own_columns(w_up))],
        "gains": lax.all_to_all(
            jnp.broadcast_to(jnp.stack([norm_gain, mlp_gain]), (members, 2, member_rows)),
            "grp",
            split_axis=0,
            concat_axis=0,
            tiled=True,
        ),
    }
    fence(e, t)
    cosine, sine = t["cos"], t["sin"]
    lag = positions[:, None] >= positions[None, :]

    def turn(pre, sign):
        half = KEY_DIM // 2
        front, back = pre[:, :half], pre[:, half:]
        return jnp.concatenate(
            [front * cosine - sign * back * sine, back * cosine + sign * front * sine], axis=1
        )

    def decayed(scores, h):
        decay = t["grow"][h][:, None] * t["shrink"][h][None, :]
        return (scores * jnp.where(lag, decay, 0.0)).astype(bf16)

    x = e["rows"].reshape(own_rows, width).astype(f32)
    gains = e.pop("gains").transpose(1, 0, 2).reshape(2, width).astype(f32)
    gain_one, gain_two = gains[0], gains[1]
    normed, norm_pullback = jax.vjp(norm_rows, x, gain_one)
    e["acts"] = normed.astype(bf16)
    e["out"] = slab_piece(e["out"])
    e["cot"] = lax.all_to_all(
        cotangent.reshape(micro, reps, strip, width), "rep", split_axis=1, concat_axis=1, tiled=True
    )
    del e["rows"]
    fence(e)
    e["acts"] = pieces_far(e["acts"])
    fence(e)
    out = Gather(padded(e.pop("out")), 0)
    tick([out])
    e["acts"] = rows_near(e["acts"])
    e["down"] = slab_piece(e["down"])
    fence(e)

    acts = e["acts"]
    weight_qkvg = assembled([(qkvg[0], 0, 0), (qkvg[1], 0, cut)], member_rows, qkvg_cols)
    tick([out])
    pre = dot(acts, weight_qkvg)
    gate_at = 2 * qk_cols + val_cols + -val_cols % 128
    value = pre[:, 2 * qk_cols : 2 * qk_cols + val_cols].astype(bf16)
    gate_pre = pre[:, gate_at : gate_at + val_cols]
    query, key = [], []
    for h in range(heads):
        query.append(turn(pre[:, h * KEY_DIM : (h + 1) * KEY_DIM], 1.0).astype(bf16))
        key.append(
            turn(pre[:, qk_cols + h * KEY_DIM : qk_cols + (h + 1) * KEY_DIM], 1.0).astype(bf16)
        )
    e = {"query": query, "cot": e["cot"], "down": e["down"], "pu": e["pu"]}
    fence(e, rings=[out])
    query = e["query"]
    tick([out])

    values, weights, mixed, tails = [], [], [], []
    for h in range(heads):
        values.append(value[:, h * VAL_DIM : (h + 1) * VAL_DIM])
        weights.append(decayed(dot_t(query[h], key[h]), h))
        retained = dot(weights[h], values[h])
        mix, pull = jax.vjp(mix_tail, retained, gate_pre[:, h * VAL_DIM : (h + 1) * VAL_DIM])
        mixed.append(mix.astype(bf16))
        tails.append(pull)
    mixed_b = padded(jnp.concatenate(mixed, axis=1))
    tick([out], free=True)
    e = {"mixed": mixed_b, "cot": e["cot"], "down": e["down"], "pu": e["pu"]}
    fence(e, rings=[out])
    pu = [Gather(e["pu"][0], 0), Gather(e["pu"][1], 1)]
    down = Gather(padded(e["down"]), 0)
    ff = pu + [down]
    tick(ff)
    mixed_b = e["mixed"]
    cot_seqs = jnp.einsum("msk,mkrd->msrd", selector, e["cot"], preferred_element_type=f32)
    cot_seqs = cot_seqs.astype(bf16).reshape(members, strip, width)
    weight_out = assembled([(out, 0, 0)], member_rows, out.part.shape[1])

    held = by_place(dot_t(mixed_b, weight_out))
    e = {"came": sum_send(held, 1), "cot": cot_seqs}
    fence(e, rings=ff)
    held = sum_take(held, e["came"], 1)
    tick(ff)
    e = {
        "sum": sum_far(held),
        "cot": lax.all_to_all(e["cot"], "grp", split_axis=0, concat_axis=0, tiled=True),
    }
    fence(e, rings=ff)

    hidden = x + e["sum"]
    out_grad = e["cot"].reshape(own_rows, width).astype(f32) * live
    normed_mid, mid_pullback = jax.vjp(norm_rows, hidden, gain_two)
    tick(ff)
    e = {"mid": pieces_far(normed_mid.astype(bf16)), "cot": out_grad.astype(bf16)}
    fence(e, rings=ff)
    tick(ff)
    e = {"mid": rows_near(e["mid"]), "cot": pieces_far(e["cot"])}
    fence(e, rings=ff)

    middle = e["mid"]
    hid = pu[0].part.shape[1]
    weight_pu = assembled([(pu[0], 0, 0), (pu[1], 0, hid)], member_rows, 2 * hid)
    pu_pre = dot(middle, weight_pu)
    proj_pre, up_pre = pu_pre[:, :hid], pu_pre[:, hid:]
    out_grad_full = rows_near(e["cot"])

    def glu_act(proj_pre, up_pre):
        return jax.nn.gelu(proj_pre, approximate=True) * up_pre

    glu_rows, glu_pullback = jax.vjp(glu_act, proj_pre, up_pre)
    glu_b = glu_rows.astype(bf16)
    ring_down = [Scatter(out_grad_full, glu_b, 0)]
    e = {"cot": out_grad_full, "glu": glu_b}
    fence(e, rings=ring_down)
    weight_down = assembled([(down, 0, 0)], member_rows, down.part.shape[1])
    tick(ring_down)
    proj_grad, up_grad = glu_pullback(dot(e["cot"], weight_down))
    pu_grad = jnp.concatenate([proj_grad, up_grad], axis=1).astype(bf16)
    held = by_place(dot_t(pu_grad, weight_pu))
    glu_b = e["glu"]
    e = {"came": sum_send(held, 1), "pu": pu_grad}
    fence(e)
    ring_ff = [Scatter(middle, e["pu"][:, :hid], 0), Scatter(middle, e["pu"][:, hid:], 1)]
    held = sum_take(held, e["came"], 1)
    tick(ring_ff)
    ring_ff = ring_ff + ring_down
    e = {"sum": sum_far(held), "glu": glu_b}
    fence(e)
    glu_b = e["glu"]

    hidden_grad = out_grad + mid_pullback(e["sum"])[0]
    tick(ring_ff)
    e = {"branch": pieces_far(hidden_grad.astype(bf16)), "glu": glu_b}
    fence(e, rings=ring_ff)
    tick(ring_ff)
    held = by_place(dot_t(e["glu"], weight_down))
    e = {"branch": rows_near(e["branch"]), "rows": sum_send(held, 1)}
    fence(e, rings=ring_ff)
    branch = e["branch"]

    mixed_grad = dot(branch, weight_out)
    retained_grads, gate_grads = [], []
    for h in range(heads):
        retained_grad, gate_grad = tails[h](mixed_grad[:, h * VAL_DIM : (h + 1) * VAL_DIM])
        retained_grads.append(retained_grad.astype(bf16))
        gate_grads.append(gate_grad.astype(bf16))
    gate_grad = padded(jnp.concatenate(gate_grads, axis=1))
    tick(ring_ff)
    held = sum_take(held, e["rows"], 1)
    ring_og = [Scatter(acts, gate_grad, 0), Scatter(branch, mixed_b, 1)]
    tick(ring_og)
    e = {"retained": retained_grads, "rows": sum_far(held)}
    fence(e, rings=ring_ff)
    retained_grads = e["retained"]
    out_rows = hidden + e["rows"]

    tick(ring_og)
    scores, value_grads = [], []
    for h in range(heads):
        scores.append(decayed(dot_t(retained_grads[h], values[h]), h))
        value_grads.append(t_dot(weights[h], retained_grads[h]).astype(bf16))
    value_grad = padded(jnp.concatenate(value_grads, axis=1))
    e = {
        "scores": scores,
        "ff": [ring.whole() for ring in ring_ff],
        "value": value_grad,
        "rows": out_rows.astype(bf16),
    }
    fence(e, rings=ring_og)
    scores, ff, value_grad = e["scores"], e["ff"], e["value"]
    ring_v = Scatter(acts, value_grad, 1)
    tick(ring_og)
    query_grads, key_grads = [], []
    for h in range(heads):
        query_grads.append(turn(dot(scores[h], key[h]), -1.0).astype(bf16))
        key_grads.append(turn(t_dot(scores[h], query[h]), -1.0).astype(bf16))
    qk_grad = jnp.concatenate(query_grads + key_grads, axis=1)
    e = {
        "grad": qk_grad,
        "pu": pieces_far(jnp.concatenate(ff[:2], axis=1)),
        "rows": lax.all_to_all(
            e["rows"].reshape(members, strip, width),
            "grp",
            split_axis=0,
            concat_axis=0,
            tiled=True,
        ),
        "down": ff[2],
    }
    fence(e, rings=ring_og)
    qk_grad, pu_far = e["grad"], e["pu"]
    out_seqs = e["rows"].reshape(micro, seqs, strip, width)
    out_bins = jnp.einsum("msk,msrd->mkrd", selector, out_seqs, preferred_element_type=f32)

    tick(ring_og + [ring_v])
    held = by_place(
        dot_t(jnp.concatenate([qk_grad, value_grad, gate_grad], axis=1), weight_qkvg)
    )
    ring_qk = Scatter(acts, qk_grad, 0)
    e = {
        "came": sum_send(held, 1),
        "pu": pieces_near(pu_far),
        "bins": lax.all_to_all(
            out_bins.astype(bf16), "rep", split_axis=1, concat_axis=1, tiled=True
        ),
        "down": e["down"],
    }
    fence(e, rings=ring_og)
    bin_out = e["bins"].reshape(micro, 1, block, width)
    held = sum_take(held, e["came"], 1)
    tick([ring_qk, ring_v])
    e = {
        "sum": sum_far(held),
        "gate": ring_og[0].whole(),
        "out": ring_og[1].whole(),
        "down": e["down"],
        "pu": e["pu"],
    }
    fence(e)
    input_grad = hidden_grad + norm_pullback(e["sum"])[0]
    tick([ring_qk, ring_v])
    e = {
        "rows": lax.all_to_all(
            input_grad.astype(bf16).reshape(members, strip, width),
            "grp",
            split_axis=0,
            concat_axis=0,
            tiled=True,
        ),
        "gate": pieces_far(e["gate"]),
        "down": slab_rows(e["down"][:, :hid_cols]),
        "out": e["out"],
        "pu": e["pu"],
    }
    fence(e, rings=[ring_qk, ring_v])
    token_grad = e["rows"].reshape(tokens.shape)

    tick([ring_qk, ring_v])
    proj_owned, up_owned, gain_two_owned = finished(
        e["pu"], ((0, hid_cols), (hid, hid_cols)), mlp_gain, (w_proj, w_up)
    )
    e = {
        "gate": pieces_near(e["gate"]),
        "slabs": pieces_far(
            jnp.concatenate([e["down"], slab_rows(e["out"][:, :val_cols])], axis=1)
        ),
        "gain": gain_two_owned,
    }
    fence(e, rings=[ring_qk, ring_v])
    gain_two_owned = e["gain"]
    tick([ring_qk])
    gate_owned, gate_sum = finished(e["gate"], ((0, val_cols),), norm_gain, (w_gate,))
    e = {
        "slabs": pieces_near(e["slabs"]),
        "gain": gate_sum,
        "last": pieces_far(jnp.concatenate([ring_qk.whole(), ring_v.whole()], axis=1)),
    }
    fence(e)
    size = width // reps
    down_owned, out_owned = finished(e["slabs"], ((0, size), (size, size)))
    query_owned, key_owned, value_owned, rest_sum = finished(
        pieces_near(e["last"]),
        ((0, qk_cols), (qk_cols, qk_cols), (2 * qk_cols, val_cols)),
        norm_gain,
        (w_query, w_key, w_value),
    )
    gain_one_owned = (e["gain"] + rest_sum)[:, 0]
    gain_two_owned = gain_two_owned[:, 0]
    return (
        bin_out,
        token_grad,
        gain_one_owned,
        query_owned,
        key_owned,
        value_owned,
        gate_owned,
        out_owned,
        gain_two_owned,
        proj_owned,
        up_owned,
        down_owned,
    )


def solution(mesh):
    return jax.shard_map(
        body,
        mesh=mesh,
        in_specs=(
            P(None, None, "grp", "rep", None),
            P(None, "rep", "grp", None),
            P(),
            P(),
            P("grp"),
            P("grp", None),
            P("grp", None),
            P("grp", None),
            P("grp", None),
            P("grp", None),
            P("grp"),
            P("grp", None),
            P("grp", None),
            P("grp", None),
        ),
        out_specs=(
            P(None, "rep", "grp", None),
            P(None, None, "grp", "rep", None),
            P("grp"),
            P("grp", None),
            P("grp", None),
            P("grp", None),
            P("grp", None),
            P("grp", None),
            P("grp"),
            P("grp", None),
            P("grp", None),
            P("grp", None),
        ),
        check_vma=False,
    )
```

```python
import functools
import math

import jax
import jax.numpy as jnp
from jax import lax
from jax.experimental import pallas as pl
from jax.experimental.pallas import tpu as pltpu
from jax.sharding import PartitionSpec as P

HEADS = 8
KEY_DIM = 256
VAL_DIM = 432

EPS = 1e-06
GROUP_EPS = 1.0

f32 = jnp.float32
bf16 = jnp.bfloat16


def norm_rows(values, gain_vec):
    return values * lax.rsqrt(jnp.mean(values * values, axis=-1, keepdims=True) + EPS) * gain_vec


def dot(left, right):
    return jnp.dot(left, right, preferred_element_type=f32)


def dot_t(left, right):
    return lax.dot_general(left, right, (((1,), (1,)), ((), ())), preferred_element_type=f32)


def t_dot(left, right):
    return lax.dot_general(left, right, (((0,), (0,)), ((), ())), preferred_element_type=f32)


def swap(value, bit):
    count = lax.axis_size("rep")
    return lax.ppermute(value, "rep", [(i, i ^ bit) for i in range(count)])


def bits_high():
    count = lax.axis_size("rep")
    return [1 << b for b in reversed(range(count.bit_length() - 1))]


latest = {}


def fence(*states, rings=(), done=()):
    leaves, tree = jax.tree.flatten(states)
    marks = [mark for ring in rings for mark in ring.marks(2)]
    marks += [mark for ring in done for mark in ring.marks(1)]
    fenced = lax.optimization_barrier((leaves, marks))[0]
    latest["mark"] = min(fenced, key=lambda leaf: leaf.size)
    for state, new in zip(states, jax.tree.unflatten(tree, fenced)):
        state.update(new)


def pieces_far(value):
    pieces = {0: value}
    for bit in bits_high()[:-1]:
        for place in list(pieces):
            pieces[place | bit] = swap(pieces[place], bit)
    return pieces


def pieces_near(pieces):
    pieces = dict(pieces)
    for place in list(pieces):
        pieces[place | 1] = swap(pieces[place], 1)
    return [pieces[place] for place in range(len(pieces))]


def pieces_of_replicas(value):
    return pieces_near(pieces_far(value))


def rows_near(pieces):
    return jnp.concatenate(pieces_near(pieces), axis=0)


def sum_send(held, bit):
    places = [o for o in held if not o & bit]
    sent = jnp.concatenate([held[o | bit].astype(bf16) for o in places], axis=0)
    return swap(sent, bit)


def sum_take(held, came, bit):
    places = [o for o in held if not o & bit]
    rows = came.shape[0] // len(places)
    return {
        o: held[o].astype(f32) + came[i * rows : (i + 1) * rows].astype(f32)
        for i, o in enumerate(places)
    }


def by_place(partial):
    count = lax.axis_size("rep")
    rows = partial.shape[0] // count
    return {o: partial[o * rows : (o + 1) * rows] for o in range(count)}


def sum_far(held):
    for bit in reversed(bits_high()[:-1]):
        held = sum_take(held, sum_send(held, bit), bit)
    return held[0]


def own_columns(weight):
    count = lax.axis_size("rep")
    width = weight.shape[1] // count
    return lax.dynamic_slice_in_dim(weight, lax.axis_index("rep") * width, width, 1)


def ring_members():
    count = lax.axis_size("grp")
    return list(range(0, count, 2)) + list(range(count - 1, 0, -2))


def ring_place():
    count, member = lax.axis_size("grp"), lax.axis_index("grp")
    return jnp.where(member % 2 == 0, member // 2, count - (member + 1) // 2)


def ring_step(value, ahead):
    ring = ring_members()
    count = len(ring)
    return lax.ppermute(
        value, "grp", [(ring[i], ring[(i + ahead) % count]) for i in range(count)]
    )


def ring_member(ahead):
    count = lax.axis_size("grp")
    place = (ring_place() + ahead) % count
    return jnp.where(place < count // 2, 2 * place, 2 * (count - place) - 1)


def gather_members(part):
    return lax.all_gather(part, "grp", axis=0, tiled=True)


def scatter_members(full):
    return lax.psum_scatter(full, "grp", scatter_dimension=0, tiled=True)


class Ring:
    def __init__(self, wide):
        half = lax.axis_size("grp") // 2
        self.left = [half if way == wide else half - 1 for way in (0, 1)]
        self.came = [[], []]

    def rest(self):
        while max(self.left) > 0:
            self.tick(free=True)

    def marks(self, back):
        return [came[-back] for came in self.came if len(came) >= back]

    def tick(self, free=False):
        for way, ahead in enumerate((1, -1)):
            if self.left[way] > 0:
                value = self.next(way, ahead)
                if not free:
                    value = lax.optimization_barrier((value, latest["mark"]))[0]
                self.came[way].append(ring_step(value, ahead))
                self.left[way] -= 1


class Gather(Ring):
    def __init__(self, part, wide):
        super().__init__(wide)
        self.part = part

    def next(self, way, ahead):
        return self.came[way][-1] if self.came[way] else self.part

    def pieces(self):
        self.rest()
        count = lax.axis_size("grp")
        pieces = {0: self.part}
        for way, ahead in enumerate((1, -1)):
            for i, came in enumerate(self.came[way]):
                pieces[-ahead * (i + 1) % count] = came
        return [pieces[i] for i in range(count)]


class Scatter(Ring):
    def __init__(self, rows, grad, wide):
        super().__init__(wide)
        self.full = t_dot(rows, grad).astype(bf16)

    def term(self, i):
        size = self.full.shape[0] // lax.axis_size("grp")
        return lax.dynamic_slice_in_dim(self.full, ring_member(i) * size, size, 0)

    def next(self, way, ahead):
        term = self.term((ahead * self.left[way]) % lax.axis_size("grp"))
        if self.came[way]:
            term = term.astype(f32) + self.came[way][-1].astype(f32)
        return term.astype(bf16)

    def whole(self):
        self.rest()
        total = self.term(0).astype(f32)
        for came in self.came:
            total = total + came[-1].astype(f32)
        return total.astype(bf16)


def assemble_kernel(spots, order_ref, *refs):
    pieces, full_ref, sems = refs[:-2], refs[-2], refs[-1]
    copies = []
    for i, (place, member_rows, row, column) in enumerate(spots):
        rows, columns = pieces[i].shape
        start = pl.multiple_of(order_ref[place] * member_rows + row, rows)
        spot = full_ref.at[pl.ds(start, rows), pl.ds(column, columns)]
        copies.append(pltpu.make_async_copy(pieces[i], spot, sems.at[i]))
    for copy in copies:
        copy.start()
    for copy in copies:
        copy.wait()


def assembled(streams, member_rows, columns):
    members = lax.axis_size("grp")
    order = jnp.stack([ring_member(i) for i in range(members)]).astype(jnp.int32)
    pieces, spots = [], []
    for gather, row, column in streams:
        for i, piece in enumerate(gather.pieces()):
            pieces.append(piece)
            spots.append((i, member_rows, row, column))
    dtype = pieces[0].dtype
    size = members * member_rows * columns * dtype.itemsize
    return pl.pallas_call(
        functools.partial(assemble_kernel, spots),
        out_shape=jax.ShapeDtypeStruct((members * member_rows, columns), dtype),
        in_specs=[pl.BlockSpec(memory_space=pltpu.SMEM)]
        + [pl.BlockSpec(memory_space=pltpu.VMEM)] * len(pieces),
        out_specs=pl.BlockSpec(memory_space=pl.ANY),
        scratch_shapes=[pltpu.SemaphoreType.DMA((len(pieces),))],
        compiler_params=pltpu.CompilerParams(vmem_limit_bytes=size + (2 << 20)),
        cost_estimate=pl.CostEstimate(flops=0, bytes_accessed=2 * size, transcendentals=0),
    )(order, *pieces)


def finish_kernel(reps, spots, summed, rank_ref, *refs):
    count = len(spots)
    pieces, refs = refs[:reps], refs[reps:]
    if summed:
        gain_ref, refs = refs[0], refs[1:]
        weights, refs = refs[:count], refs[count:]
    outs, refs = refs[:count], refs[count:]

    def lay(rank):
        for out_ref, (column, width) in zip(outs, spots):
            for r in range(reps):
                piece = pieces[rank ^ r][:, column : column + width].astype(f32)
                out_ref[:, r * width : (r + 1) * width] = piece

    for rank in range(reps):
        pl.when(rank_ref[0] == rank)(functools.partial(lay, rank))
    if summed:
        total = 0.0
        for out_ref, weight in zip(outs, weights):
            grad = out_ref[...]
            total += jnp.sum(weight[...].astype(f32) * grad, axis=1, keepdims=True)
        refs[0][...] = total / gain_ref[...].astype(f32)


def finished(pieces, spots, gain=None, weights=()):
    reps = len(pieces)
    rows, columns = pieces[0].shape
    step = rows
    for candidate in (64, 48, 72, 32):
        if rows % candidate == 0:
            step = candidate
            break
    rank = lax.axis_index("rep").astype(jnp.int32).reshape(1)

    def blocked(width):
        return pl.BlockSpec((step, width), lambda i: (i, 0))

    operands = [rank, *pieces]
    in_specs = [pl.BlockSpec(memory_space=pltpu.SMEM)] + [blocked(columns)] * reps
    shapes = [jax.ShapeDtypeStruct((rows, reps * width), f32) for _, width in spots]
    out_specs = [blocked(reps * width) for _, width in spots]
    if gain is not None:
        operands += [gain[:, None], *weights]
        in_specs += [blocked(1)] + [blocked(weight.shape[1]) for weight in weights]
        shapes.append(jax.ShapeDtypeStruct((rows, 1), f32))
        out_specs.append(blocked(1))
    size = sum(reps * width for _, width in spots) * rows
    return pl.pallas_call(
        functools.partial(finish_kernel, reps, spots, gain is not None),
        grid=(rows // step,),
        in_specs=in_specs,
        out_specs=out_specs,
        out_shape=shapes,
        compiler_params=pltpu.CompilerParams(vmem_limit_bytes=40 << 20),
        cost_estimate=pl.CostEstimate(flops=4 * size, bytes_accessed=8 * size, transcendentals=0),
    )(*operands)


def mixed_kernel(heads, q_ref, k_ref, v_ref, gate_ref, grow_ref, shrink_ref, row_ref, column_ref,
                 mixed_ref, weights_ref):
    seen = row_ref[...] >= column_ref[...]
    if mixed_ref.shape[1] > heads * VAL_DIM:
        mixed_ref[...] = jnp.zeros_like(mixed_ref)
    for h in range(heads):
        keys, cols = slice(h * KEY_DIM, (h + 1) * KEY_DIM), slice(h * VAL_DIM, (h + 1) * VAL_DIM)
        decay = jnp.where(seen, grow_ref[:, h : h + 1] * shrink_ref[h : h + 1, :], 0.0)
        weights = (dot_t(q_ref[:, keys], k_ref[:, keys]) * decay).astype(bf16)
        weights_ref[h] = weights
        retained = dot(weights, v_ref[:, cols])
        scale = lax.rsqrt(jnp.mean(retained * retained, axis=-1, keepdims=True) + GROUP_EPS)
        gate = gate_ref[:, cols]
        mixed_ref[:, cols] = (gate * jax.nn.sigmoid(gate) * (retained * scale)).astype(bf16)


def mixed_grad_kernel(heads, q_ref, k_ref, v_ref, gate_ref, grow_ref, shrink_ref, row_ref,
                      column_ref, weights_ref, grad_ref, cos_ref, sin_ref, all_cos_ref, all_sin_ref,
                      dq_ref, dgate_ref, dk_ref, dv_ref, dk_sum, dv_sum):
    seen = row_ref[...] >= column_ref[...]
    half = KEY_DIM // 2

    def turned_back(grad, cosine, sine):
        front, back = grad[:, :half], grad[:, half:]
        return front * cosine + back * sine, back * cosine - front * sine

    @pl.when(pl.program_id(0) == 0)
    def _():
        dk_sum[...] = jnp.zeros_like(dk_sum)
        dv_sum[...] = jnp.zeros_like(dv_sum)

    if dgate_ref.shape[1] > heads * VAL_DIM:
        dgate_ref[...] = jnp.zeros_like(dgate_ref)
    for h in range(heads):
        keys, cols = slice(h * KEY_DIM, (h + 1) * KEY_DIM), slice(h * VAL_DIM, (h + 1) * VAL_DIM)
        weights, value = weights_ref[h], v_ref[:, cols]
        retained = dot(weights, value)
        scale = lax.rsqrt(jnp.mean(retained * retained, axis=-1, keepdims=True) + GROUP_EPS)
        normed = retained * scale
        gate, grad = gate_ref[:, cols], grad_ref[:, cols]
        sig = jax.nn.sigmoid(gate)
        dgate_ref[:, cols] = (grad * normed * (sig * (1.0 + gate * (1.0 - sig)))).astype(bf16)
        dnormed = grad * (gate * sig)
        slope = jnp.mean(dnormed * normed, axis=-1, keepdims=True)
        dretained = (scale * (dnormed - normed * slope)).astype(bf16)
        decay = jnp.where(seen, grow_ref[:, h : h + 1] * shrink_ref[h : h + 1, :], 0.0)
        dscores = (dot_t(dretained, value) * decay).astype(bf16)
        front, back = turned_back(dot(dscores, k_ref[:, keys]), cos_ref[...], sin_ref[...])
        dq_ref[:, h * KEY_DIM : h * KEY_DIM + half] = front.astype(bf16)
        dq_ref[:, h * KEY_DIM + half : (h + 1) * KEY_DIM] = back.astype(bf16)
        dk_sum[h] += t_dot(dscores, q_ref[:, keys])
        dv_sum[h] += t_dot(weights, dretained)

    @pl.when(pl.program_id(0) == pl.num_programs(0) - 1)
    def _():
        if dv_ref.shape[1] > heads * VAL_DIM:
            dv_ref[...] = jnp.zeros_like(dv_ref)
        for h in range(heads):
            front, back = turned_back(dk_sum[h], all_cos_ref[...], all_sin_ref[...])
            dk_ref[:, h * KEY_DIM : h * KEY_DIM + half] = front.astype(bf16)
            dk_ref[:, h * KEY_DIM + half : (h + 1) * KEY_DIM] = back.astype(bf16)
            dv_ref[:, h * VAL_DIM : (h + 1) * VAL_DIM] = dv_sum[h].astype(bf16)


def retention_specs(heads, step, rows, value_cols):
    def block(width, at=0):
        return pl.BlockSpec((step, width), lambda i: (i, at))

    def whole(height, width):
        return pl.BlockSpec((height, width), lambda i: (0, 0))

    return [
        block(heads * KEY_DIM),
        whole(rows, heads * KEY_DIM),
        whole(rows, value_cols),
        block(value_cols, 1),
        block(heads),
        whole(heads, rows),
        block(1),
        whole(1, rows),
    ], block, whole


def mixed_rows(query, key, value, value_gate, tables):
    rows, value_cols = value.shape
    heads = query.shape[1] // KEY_DIM
    step = min(rows, 256)
    specs, block, _ = retention_specs(heads, step, rows, value_cols)
    return pl.pallas_call(
        functools.partial(mixed_kernel, heads),
        grid=(rows // step,),
        in_specs=specs,
        out_specs=[
            block(value_cols),
            pl.BlockSpec((heads, step, rows), lambda i: (0, i, 0)),
        ],
        out_shape=[
            jax.ShapeDtypeStruct((rows, value_cols), bf16),
            jax.ShapeDtypeStruct((heads, rows, rows), bf16),
        ],
        compiler_params=pltpu.CompilerParams(vmem_limit_bytes=48 << 20),
        cost_estimate=pl.CostEstimate(
            flops=2 * heads * rows * rows * (KEY_DIM + VAL_DIM),
            bytes_accessed=heads * rows * rows * 2 + rows * value_cols * 8,
            transcendentals=rows * value_cols,
        ),
    )(query, key, value, value_gate, *tables)


def mixed_rows_back(query, key, value, value_gate, tables, weights, grad, cosine, sine):
    rows, value_cols = value.shape
    heads = query.shape[1] // KEY_DIM
    step = min(rows, 256)
    half = KEY_DIM // 2
    specs, block, whole = retention_specs(heads, step, rows, value_cols)
    return pl.pallas_call(
        functools.partial(mixed_grad_kernel, heads),
        grid=(rows // step,),
        in_specs=specs
        + [pl.BlockSpec((heads, step, rows), lambda i: (0, i, 0)), block(value_cols)]
        + [block(half)] * 2
        + [whole(rows, half)] * 2,
        out_specs=[
            block(heads * KEY_DIM),
            block(value_cols),
            whole(rows, heads * KEY_DIM),
            whole(rows, value_cols),
        ],
        out_shape=[
            jax.ShapeDtypeStruct((rows, heads * KEY_DIM), bf16),
            jax.ShapeDtypeStruct((rows, value_cols), bf16),
            jax.ShapeDtypeStruct((rows, heads * KEY_DIM), bf16),
            jax.ShapeDtypeStruct((rows, value_cols), bf16),
        ],
        scratch_shapes=[
            pltpu.VMEM((heads, rows, KEY_DIM), f32),
            pltpu.VMEM((heads, rows, VAL_DIM), f32),
        ],
        compiler_params=pltpu.CompilerParams(vmem_limit_bytes=56 << 20),
        cost_estimate=pl.CostEstimate(
            flops=2 * heads * rows * rows * (2 * KEY_DIM + 3 * VAL_DIM),
            bytes_accessed=heads * rows * rows * 2 + rows * value_cols * 16,
            transcendentals=rows * value_cols,
        ),
    )(query, key, value, value_gate, *tables, weights, grad, cosine, sine, cosine, sine)


def slab_routes():
    reps, members = lax.axis_size("rep"), lax.axis_size("grp")
    per = members // reps
    return [
        [
            (s * members + m, (m // per) * members + per * s + (m % per + turn) % per)
            for s in range(reps)
            for m in range(members)
        ]
        for turn in range(per)
    ]


def selected(choices, which):
    result = choices[0]
    for s in range(1, len(choices)):
        result = jnp.where(which == s, choices[s], result)
    return result


def slab_parts(weight):
    reps, members = lax.axis_size("rep"), lax.axis_size("grp")
    rank, member = lax.axis_index("rep"), lax.axis_index("grp")
    per = members // reps
    size = weight.shape[1] // members
    blocks = [per * rank + (member % per + turn) % per for turn in range(per)]
    return [lax.dynamic_slice_in_dim(weight, block * size, size, 1).T for block in blocks]


def slab_piece(parts):
    reps, members = lax.axis_size("rep"), lax.axis_size("grp")
    member = lax.axis_index("grp")
    per = members // reps
    came = [
        lax.ppermute(sent, ("rep", "grp"), route) for sent, route in zip(parts, slab_routes())
    ]
    return jnp.concatenate(
        [selected([came[(e - a) % per] for e in range(per)], member % per) for a in range(per)],
        axis=1,
    )


def slab_rows(owned):
    reps, members = lax.axis_size("rep"), lax.axis_size("grp")
    member = lax.axis_index("grp")
    per = members // reps
    rows = owned.shape[1] // per
    came = []
    for turn, route in enumerate(slab_routes()):
        owner = (member % per - turn + per) % per
        sent = lax.dynamic_slice_in_dim(owned, owner * rows, rows, 1)
        came.append(lax.ppermute(sent, ("rep", "grp"), [(b, a) for a, b in route]))
    mine = jnp.concatenate(
        [
            selected([came[(k - e) % per] for e in range(per)], member % per).T
            for k in range(per)
        ],
        axis=1,
    )
    return mine


def padded(value):
    gap = -value.shape[1] % 128
    return jnp.pad(value, ((0, 0), (0, gap))) if gap else value


def body(
    tokens,
    cotangent,
    seq_lengths,
    bin_order,
    norm_gain,
    w_query,
    w_key,
    w_value,
    w_gate,
    w_out,
    mlp_gain,
    w_proj,
    w_up,
    w_down,
):
    reps, members = lax.axis_size("rep"), lax.axis_size("grp")
    rank, member = lax.axis_index("rep"), lax.axis_index("grp")
    micro, seqs, _, strip, width = tokens.shape
    own_rows = members * strip
    block = reps * strip
    heads = HEADS // reps
    qk_cols = heads * KEY_DIM
    val_cols = heads * VAL_DIM
    hid_cols = w_proj.shape[1] // reps
    member_rows = width // members

    strip_pos = (
        jnp.arange(members, dtype=jnp.int32)[:, None] * block
        + jnp.arange(strip, dtype=jnp.int32)[None, :]
    ).reshape(own_rows)
    positions = jnp.concatenate([strip_pos + strip * (rank ^ o) for o in range(reps)])
    live_len = lax.dynamic_index_in_dim(seq_lengths.reshape(-1), member, 0, False)
    live = (positions[:own_rows] < live_len).astype(f32)[:, None]
    selector = (
        bin_order[:, :, None] == jnp.arange(seqs, dtype=jnp.int32)[None, None, :]
    ).astype(bf16)

    qk = Gather(jnp.concatenate([own_columns(w_query), own_columns(w_key)], axis=1), 0)
    vg = Gather(
        jnp.concatenate([padded(own_columns(w_value)), padded(own_columns(w_gate))], axis=1), 1
    )

    def tick(rings, free=False):
        for ring in rings:
            ring.tick(free)

    frequency = jnp.exp(
        -jnp.arange(KEY_DIM // 2, dtype=f32) * (2.0 / KEY_DIM) * math.log(10000.0)
    )
    angles = positions.astype(f32)[:, None] * frequency[None, :]
    log_gamma = jnp.log(1.0 - jnp.exp2(-5.0 - (rank * heads + jnp.arange(heads)).astype(f32)))
    spans = positions.astype(f32)[None, :] * log_gamma[:, None]
    t = {
        "cos": jnp.cos(angles),
        "sin": jnp.sin(angles),
        "grow": jnp.exp(spans).T,
        "shrink": jnp.exp(-spans),
    }

    for _ in range(members // 2):
        tick([qk, vg], free=True)
    e = {
        "rows": lax.all_to_all(
            tokens.reshape(members, strip, width), "grp", split_axis=0, concat_axis=0, tiled=True
        ),
        "out": slab_parts(w_out),
        "down": slab_parts(w_down),
        "pu": [padded(own_columns(w_proj)), padded(own_columns(w_up))],
        "gains": lax.all_to_all(
            jnp.broadcast_to(jnp.stack([norm_gain, mlp_gain]), (members, 2, member_rows)),
            "grp",
            split_axis=0,
            concat_axis=0,
            tiled=True,
        ),
    }
    fence(e, t)
    cosine, sine = t["cos"], t["sin"]
    def turn(pre):
        half = KEY_DIM // 2
        front, back = pre[:, :half], pre[:, half:]
        return jnp.concatenate(
            [front * cosine - back * sine, back * cosine + front * sine], axis=1
        )

    tables = (t["grow"], t["shrink"], positions[:, None], positions[None, :])

    x = e["rows"].reshape(own_rows, width).astype(f32)
    gains = e.pop("gains").transpose(1, 0, 2).reshape(2, width).astype(f32)
    gain_one, gain_two = gains[0], gains[1]
    normed, norm_pullback = jax.vjp(norm_rows, x, gain_one)
    e["acts"] = normed.astype(bf16)
    e["out"] = slab_piece(e["out"])
    e["cot"] = lax.all_to_all(
        cotangent.reshape(micro, reps, strip, width), "rep", split_axis=1, concat_axis=1, tiled=True
    )
    del e["rows"]
    fence(e)
    e["acts"] = pieces_far(e["acts"])
    fence(e)
    out = Gather(padded(e.pop("out")), 0)
    tick([out])
    e["acts"] = rows_near(e["acts"])
    e["down"] = slab_piece(e["down"])
    fence(e)

    acts = e["acts"]
    weight_qk = assembled([(qk, 0, 0)], member_rows, 2 * qk_cols)
    tick([out])
    pre = dot(acts, weight_qk)
    def turned(at):
        parts = [
            turn(pre[:, at + h * KEY_DIM : at + (h + 1) * KEY_DIM]).astype(bf16)
            for h in range(heads)
        ]
        return jnp.concatenate(parts, axis=1)

    query, key = turned(0), turned(qk_cols)
    e = {
        "query": query,
        "key": key,
        "cot": e["cot"],
        "down": e["down"],
        "pu": e["pu"],
        "acts": acts,
    }
    fence(e, done=[vg])
    query, key, acts = e["query"], e["key"], e["acts"]
    weight_vg = assembled([(vg, 0, 0)], member_rows, vg.part.shape[1])
    tick([out])
    gate_at = vg.part.shape[1] // 2
    value_gate = dot(acts, weight_vg)
    e = {
        "cot": e["cot"],
        "down": e["down"],
        "pu": e["pu"],
        "value": value_gate[:, :gate_at].astype(bf16),
    }
    fence(e, done=[out])
    value = e["value"]
    tick([out])

    mixed_b, weights = mixed_rows(query, key, value, value_gate, tables)
    tick([out], free=True)
    pu = [Gather(e["pu"][0], 0), Gather(e["pu"][1], 1)]
    tick(pu)
    e = {"mixed": mixed_b, "cot": e["cot"], "down": e["down"]}
    fence(e, done=[out] + pu)
    tick(pu)
    down = Gather(padded(e["down"]), 0)
    mixed_b = e["mixed"]
    cot_seqs = jnp.einsum("msk,mkrd->msrd", selector, e["cot"], preferred_element_type=f32)
    cot_seqs = cot_seqs.astype(bf16).reshape(members, strip, width)
    weight_out = assembled([(out, 0, 0)], member_rows, out.part.shape[1])

    held = by_place(dot_t(mixed_b, weight_out))
    e = {"came": sum_send(held, 1), "cot": cot_seqs}
    fence(e, done=pu)
    held = sum_take(held, e["came"], 1)
    tick(pu)
    e = {
        "sum": sum_far(held),
        "cot": lax.all_to_all(e["cot"], "grp", split_axis=0, concat_axis=0, tiled=True),
    }
    fence(e, done=pu)

    hidden = x + e["sum"]
    out_grad = e["cot"].reshape(own_rows, width).astype(f32) * live
    normed_mid, mid_pullback = jax.vjp(norm_rows, hidden, gain_two)
    tick(pu + [down])
    e = {"mid": pieces_far(normed_mid.astype(bf16)), "cot": out_grad.astype(bf16)}
    fence(e, done=pu + [down])
    tick([down])
    e = {"mid": rows_near(e["mid"]), "cot": pieces_far(e["cot"])}
    fence(e, rings=[down])

    middle = e["mid"]
    hid = pu[0].part.shape[1]
    weight_pu = assembled([(pu[0], 0, 0), (pu[1], 0, hid)], member_rows, 2 * hid)
    pu_pre = dot(middle, weight_pu)
    proj_pre, up_pre = pu_pre[:, :hid], pu_pre[:, hid:]
    out_grad_full = rows_near(e["cot"])

    def glu_act(proj_pre, up_pre):
        return jax.nn.gelu(proj_pre, approximate=True) * up_pre

    glu_rows, glu_pullback = jax.vjp(glu_act, proj_pre, up_pre)
    glu_b = glu_rows.astype(bf16)
    tick([down])
    ring_down = [Scatter(out_grad_full, glu_b, 0)]
    e = {"cot": out_grad_full, "glu": glu_b}
    fence(e, done=[down])
    tick([down])
    weight_down = assembled([(down, 0, 0)], member_rows, down.part.shape[1])
    proj_grad, up_grad = glu_pullback(dot(e["cot"], weight_down))
    pu_grad = jnp.concatenate([proj_grad, up_grad], axis=1).astype(bf16)
    held = by_place(dot_t(pu_grad, weight_pu))
    glu_b = e["glu"]
    e = {"came": sum_send(held, 1), "pu": pu_grad}
    fence(e)
    ring_ff = [Scatter(middle, e["pu"][:, :hid], 0), Scatter(middle, e["pu"][:, hid:], 1)]
    held = sum_take(held, e["came"], 1)
    tick(ring_ff)
    ring_ff = ring_ff + ring_down
    e = {"sum": sum_far(held), "glu": glu_b}
    fence(e)
    glu_b = e["glu"]

    hidden_grad = out_grad + mid_pullback(e["sum"])[0]
    tick(ring_ff)
    e = {"branch": pieces_far(hidden_grad.astype(bf16)), "glu": glu_b}
    fence(e, rings=ring_ff)
    tick(ring_ff)
    held = by_place(dot_t(e["glu"], weight_down))
    e = {"branch": rows_near(e["branch"]), "rows": sum_send(held, 1)}
    fence(e, rings=ring_ff)
    branch = e["branch"]

    mixed_grad = dot(branch, weight_out)
    query_grad, gate_grad, key_grad, value_grad = mixed_rows_back(
        query, key, value, value_gate, tables, weights, mixed_grad, cosine, sine
    )
    tick(ring_ff)
    held = sum_take(held, e["rows"], 1)
    ring_og = [Scatter(acts, gate_grad, 0), Scatter(branch, mixed_b, 1)]
    tick(ring_og)
    e = {
        "qk": jnp.concatenate([query_grad, key_grad], axis=1),
        "value": value_grad,
        "gate": gate_grad,
        "rows": sum_far(held),
    }
    fence(e, rings=ring_ff)
    qk_grad, value_grad, gate_grad = e["qk"], e["value"], e["gate"]
    out_rows = hidden + e["rows"]
    tick(ring_og)
    ff = [ring.whole() for ring in ring_ff]
    ring_v = Scatter(acts, value_grad, 1)
    ring_qk = Scatter(acts, qk_grad, 0)
    e = {
        "qk": qk_grad,
        "full": [ring_v.full, ring_qk.full],
        "pu": pieces_far(jnp.concatenate(ff[:2], axis=1)),
        "rows": lax.all_to_all(
            out_rows.astype(bf16).reshape(members, strip, width),
            "grp",
            split_axis=0,
            concat_axis=0,
            tiled=True,
        ),
        "down": ff[2],
    }
    fence(e, rings=ring_og)
    qk_grad, pu_far = e["qk"], e["pu"]
    ring_v.full, ring_qk.full = e["full"]
    out_seqs = e["rows"].reshape(micro, seqs, strip, width)
    out_bins = jnp.einsum("msk,msrd->mkrd", selector, out_seqs, preferred_element_type=f32)

    tick(ring_og + [ring_v, ring_qk])
    vg_grad = jnp.concatenate([value_grad, gate_grad], axis=1)
    held = by_place(dot_t(qk_grad, weight_qk) + dot_t(vg_grad, weight_vg))
    e = {
        "came": sum_send(held, 1),
        "pu": pieces_near(pu_far),
        "bins": lax.all_to_all(
            out_bins.astype(bf16), "rep", split_axis=1, concat_axis=1, tiled=True
        ),
        "down": slab_rows(e["down"][:, :hid_cols]),
    }
    fence(e, rings=ring_og)
    bin_out = e["bins"].reshape(micro, 1, block, width)
    held = sum_take(held, e["came"], 1)
    tick(ring_og + [ring_v, ring_qk])
    e = {"sum": sum_far(held), "down": e["down"], "pu": e["pu"]}
    fence(e, rings=[ring_v, ring_qk], done=ring_og)
    gate_part, out_mine = ring_og[0].whole(), slab_rows(ring_og[1].whole()[:, :val_cols])
    input_grad = hidden_grad + norm_pullback(e["sum"])[0]
    tick([ring_v, ring_qk])
    e = {
        "rows": lax.all_to_all(
            input_grad.astype(bf16).reshape(members, strip, width),
            "grp",
            split_axis=0,
            concat_axis=0,
            tiled=True,
        ),
        "gate": pieces_far(gate_part),
        "slabs": jnp.concatenate([e["down"], out_mine], axis=1),
        "pu": e["pu"],
    }
    fence(e, rings=[ring_v, ring_qk])
    token_grad = e["rows"].reshape(tokens.shape)

    tick([ring_v, ring_qk])
    proj_owned, up_owned, gain_two_owned = finished(
        e["pu"], ((0, hid_cols), (hid, hid_cols)), mlp_gain, (w_proj, w_up)
    )
    e = {
        "gate": pieces_near(e["gate"]),
        "slabs": pieces_far(e["slabs"]),
        "gain": gain_two_owned,
    }
    fence(e, done=[ring_v, ring_qk])
    gain_two_owned = e["gain"]
    gate_owned, gate_sum = finished(e["gate"], ((0, val_cols),), norm_gain, (w_gate,))
    e = {
        "slabs": pieces_near(e["slabs"]),
        "last": pieces_far(jnp.concatenate([ring_qk.whole(), ring_v.whole()], axis=1)),
        "gain": gate_sum,
    }
    fence(e)
    size = width // reps
    down_owned, out_owned = finished(e["slabs"], ((0, size), (size, size)))
    query_owned, key_owned, value_owned, rest_sum = finished(
        pieces_near(e["last"]),
        ((0, qk_cols), (qk_cols, qk_cols), (2 * qk_cols, val_cols)),
        norm_gain,
        (w_query, w_key, w_value),
    )
    gain_one_owned = (e["gain"] + rest_sum)[:, 0]
    gain_two_owned = gain_two_owned[:, 0]
    return (
        bin_out,
        token_grad,
        gain_one_owned,
        query_owned,
        key_owned,
        value_owned,
        gate_owned,
        out_owned,
        gain_two_owned,
        proj_owned,
        up_owned,
        down_owned,
    )


def solution(mesh):
    return jax.shard_map(
        body,
        mesh=mesh,
        in_specs=(
            P(None, None, "grp", "rep", None),
            P(None, "rep", "grp", None),
            P(),
            P(),
            P("grp"),
            P("grp", None),
            P("grp", None),
            P("grp", None),
            P("grp", None),
            P("grp", None),
            P("grp"),
            P("grp", None),
            P("grp", None),
            P("grp", None),
        ),
        out_specs=(
            P(None, "rep", "grp", None),
            P(None, None, "grp", "rep", None),
            P("grp"),
            P("grp", None),
            P("grp", None),
            P("grp", None),
            P("grp", None),
            P("grp", None),
            P("grp"),
            P("grp", None),
            P("grp", None),
            P("grp", None),
        ),
        check_vma=False,
    )
```

```python
import functools
import math

import jax
import jax.numpy as jnp
from jax import lax
from jax.experimental import pallas as pl
from jax.experimental.pallas import tpu as pltpu
from jax.sharding import PartitionSpec as P

HEADS = 8
KEY_DIM = 256
VAL_DIM = 432

EPS = 1e-06
GROUP_EPS = 1.0

f32 = jnp.float32
bf16 = jnp.bfloat16


def norm_rows(values, gain_vec):
    return values * lax.rsqrt(jnp.mean(values * values, axis=-1, keepdims=True) + EPS) * gain_vec


def dot(left, right):
    return jnp.dot(left, right, preferred_element_type=f32)


def dot_t(left, right):
    return lax.dot_general(left, right, (((1,), (1,)), ((), ())), preferred_element_type=f32)


def t_dot(left, right):
    return lax.dot_general(left, right, (((0,), (0,)), ((), ())), preferred_element_type=f32)


def swap(value, bit):
    count = lax.axis_size("rep")
    return lax.ppermute(value, "rep", [(i, i ^ bit) for i in range(count)])


def bits_high():
    count = lax.axis_size("rep")
    return [1 << b for b in reversed(range(count.bit_length() - 1))]


latest = {}


def fence(*states, rings=(), done=()):
    leaves, tree = jax.tree.flatten(states)
    marks = [mark for ring in rings for mark in ring.marks(2)]
    marks += [mark for ring in done for mark in ring.marks(1)]
    fenced = lax.optimization_barrier((leaves, marks))[0]
    latest["mark"] = min(fenced, key=lambda leaf: leaf.size)
    for state, new in zip(states, jax.tree.unflatten(tree, fenced)):
        state.update(new)


def pieces_far(value):
    pieces = {0: value}
    for bit in bits_high()[:-1]:
        for place in list(pieces):
            pieces[place | bit] = swap(pieces[place], bit)
    return pieces


def pieces_near(pieces):
    pieces = dict(pieces)
    for place in list(pieces):
        pieces[place | 1] = swap(pieces[place], 1)
    return [pieces[place] for place in range(len(pieces))]


def pieces_of_replicas(value):
    return pieces_near(pieces_far(value))


def rows_near(pieces):
    return jnp.concatenate(pieces_near(pieces), axis=0)


def sum_send(held, bit):
    places = [o for o in held if not o & bit]
    sent = jnp.concatenate([held[o | bit].astype(bf16) for o in places], axis=0)
    return swap(sent, bit)


def sum_take(held, came, bit):
    places = [o for o in held if not o & bit]
    rows = came.shape[0] // len(places)
    return {
        o: held[o].astype(f32) + came[i * rows : (i + 1) * rows].astype(f32)
        for i, o in enumerate(places)
    }


def by_place(partial):
    count = lax.axis_size("rep")
    rows = partial.shape[0] // count
    return {o: partial[o * rows : (o + 1) * rows] for o in range(count)}


def sum_far(held):
    for bit in reversed(bits_high()[:-1]):
        held = sum_take(held, sum_send(held, bit), bit)
    return held[0]


def own_columns(weight):
    count = lax.axis_size("rep")
    width = weight.shape[1] // count
    return lax.dynamic_slice_in_dim(weight, lax.axis_index("rep") * width, width, 1)


def ring_members():
    count = lax.axis_size("grp")
    return list(range(0, count, 2)) + list(range(count - 1, 0, -2))


def ring_place():
    count, member = lax.axis_size("grp"), lax.axis_index("grp")
    return jnp.where(member % 2 == 0, member // 2, count - (member + 1) // 2)


def ring_step(value, ahead):
    ring = ring_members()
    count = len(ring)
    return lax.ppermute(
        value, "grp", [(ring[i], ring[(i + ahead) % count]) for i in range(count)]
    )


def ring_member(ahead):
    count = lax.axis_size("grp")
    place = (ring_place() + ahead) % count
    return jnp.where(place < count // 2, 2 * place, 2 * (count - place) - 1)


def gather_members(part):
    return lax.all_gather(part, "grp", axis=0, tiled=True)


def scatter_members(full):
    return lax.psum_scatter(full, "grp", scatter_dimension=0, tiled=True)


class Ring:
    def __init__(self, wide):
        half = lax.axis_size("grp") // 2
        self.left = [half if way == wide else half - 1 for way in (0, 1)]
        self.came = [[], []]

    def rest(self):
        while max(self.left) > 0:
            self.tick(free=True)

    def marks(self, back):
        return [came[-back] for came in self.came if len(came) >= back]

    def tick(self, free=False):
        for way, ahead in enumerate((1, -1)):
            if self.left[way] > 0:
                value = self.next(way, ahead)
                if not free:
                    value = lax.optimization_barrier((value, latest["mark"]))[0]
                self.came[way].append(ring_step(value, ahead))
                self.left[way] -= 1


class Gather(Ring):
    def __init__(self, part, wide):
        super().__init__(wide)
        self.part = part

    def next(self, way, ahead):
        return self.came[way][-1] if self.came[way] else self.part

    def pieces(self):
        self.rest()
        count = lax.axis_size("grp")
        pieces = {0: self.part}
        for way, ahead in enumerate((1, -1)):
            for i, came in enumerate(self.came[way]):
                pieces[-ahead * (i + 1) % count] = came
        return [pieces[i] for i in range(count)]


class Scatter(Ring):
    def __init__(self, rows, grad, wide):
        super().__init__(wide)
        self.full = t_dot(rows, grad).astype(bf16)

    def term(self, i):
        size = self.full.shape[0] // lax.axis_size("grp")
        return lax.dynamic_slice_in_dim(self.full, ring_member(i) * size, size, 0)

    def next(self, way, ahead):
        term = self.term((ahead * self.left[way]) % lax.axis_size("grp"))
        if self.came[way]:
            term = term.astype(f32) + self.came[way][-1].astype(f32)
        return term.astype(bf16)

    def whole(self):
        self.rest()
        total = self.term(0).astype(f32)
        for came in self.came:
            total = total + came[-1].astype(f32)
        return total.astype(bf16)


def assemble_kernel(spots, order_ref, *refs):
    pieces, full_ref, sems = refs[:-2], refs[-2], refs[-1]
    copies = []
    for i, (place, member_rows, row, column) in enumerate(spots):
        rows, columns = pieces[i].shape
        start = pl.multiple_of(order_ref[place] * member_rows + row, rows)
        spot = full_ref.at[pl.ds(start, rows), pl.ds(column, columns)]
        copies.append(pltpu.make_async_copy(pieces[i], spot, sems.at[i]))
    for copy in copies:
        copy.start()
    for copy in copies:
        copy.wait()


def assembled(streams, member_rows, columns):
    members = lax.axis_size("grp")
    order = jnp.stack([ring_member(i) for i in range(members)]).astype(jnp.int32)
    pieces, spots = [], []
    for gather, row, column in streams:
        for i, piece in enumerate(gather.pieces()):
            pieces.append(piece)
            spots.append((i, member_rows, row, column))
    dtype = pieces[0].dtype
    size = members * member_rows * columns * dtype.itemsize
    return pl.pallas_call(
        functools.partial(assemble_kernel, spots),
        out_shape=jax.ShapeDtypeStruct((members * member_rows, columns), dtype),
        in_specs=[pl.BlockSpec(memory_space=pltpu.SMEM)]
        + [pl.BlockSpec(memory_space=pltpu.VMEM)] * len(pieces),
        out_specs=pl.BlockSpec(memory_space=pl.ANY),
        scratch_shapes=[pltpu.SemaphoreType.DMA((len(pieces),))],
        compiler_params=pltpu.CompilerParams(vmem_limit_bytes=size + (2 << 20)),
        cost_estimate=pl.CostEstimate(flops=0, bytes_accessed=2 * size, transcendentals=0),
    )(order, *pieces)


def finish_kernel(reps, spots, summed, rank_ref, *refs):
    count = len(spots)
    pieces, refs = refs[:reps], refs[reps:]
    if summed:
        gain_ref, refs = refs[0], refs[1:]
        weights, refs = refs[:count], refs[count:]
    outs, refs = refs[:count], refs[count:]

    def lay(rank):
        for out_ref, (column, width) in zip(outs, spots):
            for r in range(reps):
                piece = pieces[rank ^ r][:, column : column + width].astype(f32)
                out_ref[:, r * width : (r + 1) * width] = piece

    for rank in range(reps):
        pl.when(rank_ref[0] == rank)(functools.partial(lay, rank))
    if summed:
        total = 0.0
        for out_ref, weight in zip(outs, weights):
            grad = out_ref[...]
            total += jnp.sum(weight[...].astype(f32) * grad, axis=1, keepdims=True)
        refs[0][...] = total / gain_ref[...].astype(f32)


def finished(pieces, spots, gain=None, weights=()):
    reps = len(pieces)
    rows, columns = pieces[0].shape
    step = rows
    for candidate in (64, 48, 72, 32):
        if rows % candidate == 0:
            step = candidate
            break
    rank = lax.axis_index("rep").astype(jnp.int32).reshape(1)

    def blocked(width):
        return pl.BlockSpec((step, width), lambda i: (i, 0))

    operands = [rank, *pieces]
    in_specs = [pl.BlockSpec(memory_space=pltpu.SMEM)] + [blocked(columns)] * reps
    shapes = [jax.ShapeDtypeStruct((rows, reps * width), f32) for _, width in spots]
    out_specs = [blocked(reps * width) for _, width in spots]
    if gain is not None:
        operands += [gain[:, None], *weights]
        in_specs += [blocked(1)] + [blocked(weight.shape[1]) for weight in weights]
        shapes.append(jax.ShapeDtypeStruct((rows, 1), f32))
        out_specs.append(blocked(1))
    size = sum(reps * width for _, width in spots) * rows
    return pl.pallas_call(
        functools.partial(finish_kernel, reps, spots, gain is not None),
        grid=(rows // step,),
        in_specs=in_specs,
        out_specs=out_specs,
        out_shape=shapes,
        compiler_params=pltpu.CompilerParams(vmem_limit_bytes=40 << 20),
        cost_estimate=pl.CostEstimate(flops=4 * size, bytes_accessed=8 * size, transcendentals=0),
    )(*operands)


def mixed_kernel(heads, q_ref, k_ref, v_ref, gate_ref, grow_ref, shrink_ref, row_ref, column_ref,
                 mixed_ref, weights_ref):
    seen = row_ref[...] >= column_ref[...]
    if mixed_ref.shape[1] > heads * VAL_DIM:
        mixed_ref[...] = jnp.zeros_like(mixed_ref)
    for h in range(heads):
        keys, cols = slice(h * KEY_DIM, (h + 1) * KEY_DIM), slice(h * VAL_DIM, (h + 1) * VAL_DIM)
        decay = jnp.where(seen, grow_ref[:, h : h + 1] * shrink_ref[h : h + 1, :], 0.0)
        weights = (dot_t(q_ref[:, keys], k_ref[:, keys]) * decay).astype(bf16)
        weights_ref[h] = weights
        retained = dot(weights, v_ref[:, cols])
        scale = lax.rsqrt(jnp.mean(retained * retained, axis=-1, keepdims=True) + GROUP_EPS)
        gate = gate_ref[:, cols]
        mixed_ref[:, cols] = (gate * jax.nn.sigmoid(gate) * (retained * scale)).astype(bf16)


def mixed_grad_kernel(heads, q_ref, k_ref, v_ref, gate_ref, grow_ref, shrink_ref, row_ref,
                      column_ref, weights_ref, grad_ref, cos_ref, sin_ref, all_cos_ref, all_sin_ref,
                      dq_ref, dgate_ref, dk_ref, dv_ref, dk_sum, dv_sum):
    seen = row_ref[...] >= column_ref[...]
    half = KEY_DIM // 2

    def turned_back(grad, cosine, sine):
        front, back = grad[:, :half], grad[:, half:]
        return front * cosine + back * sine, back * cosine - front * sine

    @pl.when(pl.program_id(0) == 0)
    def _():
        dk_sum[...] = jnp.zeros_like(dk_sum)
        dv_sum[...] = jnp.zeros_like(dv_sum)

    if dgate_ref.shape[1] > heads * VAL_DIM:
        dgate_ref[...] = jnp.zeros_like(dgate_ref)
    for h in range(heads):
        keys, cols = slice(h * KEY_DIM, (h + 1) * KEY_DIM), slice(h * VAL_DIM, (h + 1) * VAL_DIM)
        weights, value = weights_ref[h], v_ref[:, cols]
        retained = dot(weights, value)
        scale = lax.rsqrt(jnp.mean(retained * retained, axis=-1, keepdims=True) + GROUP_EPS)
        normed = retained * scale
        gate, grad = gate_ref[:, cols], grad_ref[:, cols]
        sig = jax.nn.sigmoid(gate)
        dgate_ref[:, cols] = (grad * normed * (sig * (1.0 + gate * (1.0 - sig)))).astype(bf16)
        dnormed = grad * (gate * sig)
        slope = jnp.mean(dnormed * normed, axis=-1, keepdims=True)
        dretained = (scale * (dnormed - normed * slope)).astype(bf16)
        decay = jnp.where(seen, grow_ref[:, h : h + 1] * shrink_ref[h : h + 1, :], 0.0)
        dscores = (dot_t(dretained, value) * decay).astype(bf16)
        front, back = turned_back(dot(dscores, k_ref[:, keys]), cos_ref[...], sin_ref[...])
        dq_ref[:, h * KEY_DIM : h * KEY_DIM + half] = front.astype(bf16)
        dq_ref[:, h * KEY_DIM + half : (h + 1) * KEY_DIM] = back.astype(bf16)
        dk_sum[h] += t_dot(dscores, q_ref[:, keys])
        dv_sum[h] += t_dot(weights, dretained)

    @pl.when(pl.program_id(0) == pl.num_programs(0) - 1)
    def _():
        if dv_ref.shape[1] > heads * VAL_DIM:
            dv_ref[...] = jnp.zeros_like(dv_ref)
        for h in range(heads):
            front, back = turned_back(dk_sum[h], all_cos_ref[...], all_sin_ref[...])
            dk_ref[:, h * KEY_DIM : h * KEY_DIM + half] = front.astype(bf16)
            dk_ref[:, h * KEY_DIM + half : (h + 1) * KEY_DIM] = back.astype(bf16)
            dv_ref[:, h * VAL_DIM : (h + 1) * VAL_DIM] = dv_sum[h].astype(bf16)


def retention_specs(heads, step, rows, value_cols):
    def block(width, at=0):
        return pl.BlockSpec((step, width), lambda i: (i, at))

    def whole(height, width):
        return pl.BlockSpec((height, width), lambda i: (0, 0))

    return [
        block(heads * KEY_DIM),
        whole(rows, heads * KEY_DIM),
        whole(rows, value_cols),
        block(value_cols, 1),
        block(heads),
        whole(heads, rows),
        block(1),
        whole(1, rows),
    ], block, whole


def mixed_rows(query, key, value, value_gate, tables):
    rows, value_cols = value.shape
    heads = query.shape[1] // KEY_DIM
    step = min(rows, 256)
    specs, block, _ = retention_specs(heads, step, rows, value_cols)
    return pl.pallas_call(
        functools.partial(mixed_kernel, heads),
        grid=(rows // step,),
        in_specs=specs,
        out_specs=[
            block(value_cols),
            pl.BlockSpec((heads, step, rows), lambda i: (0, i, 0)),
        ],
        out_shape=[
            jax.ShapeDtypeStruct((rows, value_cols), bf16),
            jax.ShapeDtypeStruct((heads, rows, rows), bf16),
        ],
        compiler_params=pltpu.CompilerParams(vmem_limit_bytes=48 << 20),
        cost_estimate=pl.CostEstimate(
            flops=2 * heads * rows * rows * (KEY_DIM + VAL_DIM),
            bytes_accessed=heads * rows * rows * 2 + rows * value_cols * 8,
            transcendentals=rows * value_cols,
        ),
    )(query, key, value, value_gate, *tables)


def mixed_rows_back(query, key, value, value_gate, tables, weights, grad, cosine, sine):
    rows, value_cols = value.shape
    heads = query.shape[1] // KEY_DIM
    step = min(rows, 256)
    half = KEY_DIM // 2
    specs, block, whole = retention_specs(heads, step, rows, value_cols)
    return pl.pallas_call(
        functools.partial(mixed_grad_kernel, heads),
        grid=(rows // step,),
        in_specs=specs
        + [pl.BlockSpec((heads, step, rows), lambda i: (0, i, 0)), block(value_cols)]
        + [block(half)] * 2
        + [whole(rows, half)] * 2,
        out_specs=[
            block(heads * KEY_DIM),
            block(value_cols),
            whole(rows, heads * KEY_DIM),
            whole(rows, value_cols),
        ],
        out_shape=[
            jax.ShapeDtypeStruct((rows, heads * KEY_DIM), bf16),
            jax.ShapeDtypeStruct((rows, value_cols), bf16),
            jax.ShapeDtypeStruct((rows, heads * KEY_DIM), bf16),
            jax.ShapeDtypeStruct((rows, value_cols), bf16),
        ],
        scratch_shapes=[
            pltpu.VMEM((heads, rows, KEY_DIM), f32),
            pltpu.VMEM((heads, rows, VAL_DIM), f32),
        ],
        compiler_params=pltpu.CompilerParams(vmem_limit_bytes=56 << 20),
        cost_estimate=pl.CostEstimate(
            flops=2 * heads * rows * rows * (2 * KEY_DIM + 3 * VAL_DIM),
            bytes_accessed=heads * rows * rows * 2 + rows * value_cols * 16,
            transcendentals=rows * value_cols,
        ),
    )(query, key, value, value_gate, *tables, weights, grad, cosine, sine, cosine, sine)


def slab_routes():
    reps, members = lax.axis_size("rep"), lax.axis_size("grp")
    per = members // reps
    return [
        [
            (s * members + m, (m // per) * members + per * s + (m % per + turn) % per)
            for s in range(reps)
            for m in range(members)
        ]
        for turn in range(per)
    ]


def selected(choices, which):
    result = choices[0]
    for s in range(1, len(choices)):
        result = jnp.where(which == s, choices[s], result)
    return result


def slab_parts(weight):
    reps, members = lax.axis_size("rep"), lax.axis_size("grp")
    rank, member = lax.axis_index("rep"), lax.axis_index("grp")
    per = members // reps
    size = weight.shape[1] // members
    blocks = [per * rank + (member % per + turn) % per for turn in range(per)]
    return [lax.dynamic_slice_in_dim(weight, block * size, size, 1).T for block in blocks]


def slab_piece(parts):
    reps, members = lax.axis_size("rep"), lax.axis_size("grp")
    member = lax.axis_index("grp")
    per = members // reps
    came = [
        lax.ppermute(sent, ("rep", "grp"), route) for sent, route in zip(parts, slab_routes())
    ]
    return jnp.concatenate(
        [selected([came[(e - a) % per] for e in range(per)], member % per) for a in range(per)],
        axis=1,
    )


def slab_rows(owned):
    reps, members = lax.axis_size("rep"), lax.axis_size("grp")
    member = lax.axis_index("grp")
    per = members // reps
    rows = owned.shape[1] // per
    came = []
    for turn, route in enumerate(slab_routes()):
        owner = (member % per - turn + per) % per
        sent = lax.dynamic_slice_in_dim(owned, owner * rows, rows, 1)
        came.append(lax.ppermute(sent, ("rep", "grp"), [(b, a) for a, b in route]))
    mine = jnp.concatenate(
        [
            selected([came[(k - e) % per] for e in range(per)], member % per).T
            for k in range(per)
        ],
        axis=1,
    )
    return mine


def padded(value):
    gap = -value.shape[1] % 128
    return jnp.pad(value, ((0, 0), (0, gap))) if gap else value


def body(
    tokens,
    cotangent,
    seq_lengths,
    bin_order,
    norm_gain,
    w_query,
    w_key,
    w_value,
    w_gate,
    w_out,
    mlp_gain,
    w_proj,
    w_up,
    w_down,
):
    reps, members = lax.axis_size("rep"), lax.axis_size("grp")
    rank, member = lax.axis_index("rep"), lax.axis_index("grp")
    micro, seqs, _, strip, width = tokens.shape
    own_rows = members * strip
    block = reps * strip
    heads = HEADS // reps
    qk_cols = heads * KEY_DIM
    val_cols = heads * VAL_DIM
    hid_cols = w_proj.shape[1] // reps
    member_rows = width // members

    strip_pos = (
        jnp.arange(members, dtype=jnp.int32)[:, None] * block
        + jnp.arange(strip, dtype=jnp.int32)[None, :]
    ).reshape(own_rows)
    positions = jnp.concatenate([strip_pos + strip * (rank ^ o) for o in range(reps)])
    live_len = lax.dynamic_index_in_dim(seq_lengths.reshape(-1), member, 0, False)
    live = (positions[:own_rows] < live_len).astype(f32)[:, None]
    selector = (
        bin_order[:, :, None] == jnp.arange(seqs, dtype=jnp.int32)[None, None, :]
    ).astype(bf16)

    qk = Gather(jnp.concatenate([own_columns(w_query), own_columns(w_key)], axis=1), 0)
    vg = Gather(
        jnp.concatenate([padded(own_columns(w_value)), padded(own_columns(w_gate))], axis=1), 1
    )

    def tick(rings, free=False):
        for ring in rings:
            ring.tick(free)

    frequency = jnp.exp(
        -jnp.arange(KEY_DIM // 2, dtype=f32) * (2.0 / KEY_DIM) * math.log(10000.0)
    )
    angles = positions.astype(f32)[:, None] * frequency[None, :]
    log_gamma = jnp.log(1.0 - jnp.exp2(-5.0 - (rank * heads + jnp.arange(heads)).astype(f32)))
    spans = positions.astype(f32)[None, :] * log_gamma[:, None]
    t = {
        "cos": jnp.cos(angles),
        "sin": jnp.sin(angles),
        "grow": jnp.exp(spans).T,
        "shrink": jnp.exp(-spans),
    }

    for _ in range(members // 2):
        tick([qk, vg], free=True)
    e = {
        "rows": lax.all_to_all(
            tokens.reshape(members, strip, width), "grp", split_axis=0, concat_axis=0, tiled=True
        ),
        "out": slab_parts(w_out),
        "down": slab_parts(w_down),
        "pu": [padded(own_columns(w_proj)), padded(own_columns(w_up))],
        "gains": lax.all_to_all(
            jnp.broadcast_to(jnp.stack([norm_gain, mlp_gain]), (members, 2, member_rows)),
            "grp",
            split_axis=0,
            concat_axis=0,
            tiled=True,
        ),
    }
    fence(e, t)
    cosine, sine = t["cos"], t["sin"]
    def turn(pre):
        half = KEY_DIM // 2
        front, back = pre[:, :half], pre[:, half:]
        return jnp.concatenate(
            [front * cosine - back * sine, back * cosine + front * sine], axis=1
        )

    tables = (t["grow"], t["shrink"], positions[:, None], positions[None, :])

    x = e["rows"].reshape(own_rows, width).astype(f32)
    gains = e.pop("gains").transpose(1, 0, 2).reshape(2, width).astype(f32)
    gain_one, gain_two = gains[0], gains[1]
    normed, norm_pullback = jax.vjp(norm_rows, x, gain_one)
    e["acts"] = normed.astype(bf16)
    e["cot"] = lax.all_to_all(
        cotangent.reshape(micro, reps, strip, width), "rep", split_axis=1, concat_axis=1, tiled=True
    )
    del e["rows"]
    fence(e)
    e["acts"] = pieces_far(e["acts"])
    fence(e)
    e["acts"] = rows_near(e["acts"])
    e["out"] = slab_piece(e["out"])
    fence(e)
    out = Gather(padded(e.pop("out")), 0)

    acts = e["acts"]
    weight_qk = assembled([(qk, 0, 0)], member_rows, 2 * qk_cols)
    tick([out])
    pre = dot(acts, weight_qk)
    def turned(at):
        parts = [
            turn(pre[:, at + h * KEY_DIM : at + (h + 1) * KEY_DIM]).astype(bf16)
            for h in range(heads)
        ]
        return jnp.concatenate(parts, axis=1)

    query, key = turned(0), turned(qk_cols)
    e = {
        "query": query,
        "key": key,
        "cot": e["cot"],
        "down": e["down"],
        "pu": e["pu"],
        "acts": acts,
    }
    fence(e, done=[vg])
    query, key, acts = e["query"], e["key"], e["acts"]
    weight_vg = assembled([(vg, 0, 0)], member_rows, vg.part.shape[1])
    tick([out])
    gate_at = vg.part.shape[1] // 2
    value_gate = dot(acts, weight_vg)
    e = {
        "cot": e["cot"],
        "down": slab_piece(e["down"]),
        "pu": e["pu"],
        "value": value_gate[:, :gate_at].astype(bf16),
    }
    fence(e, done=[out])
    value = e["value"]
    tick([out])

    mixed_b, weights = mixed_rows(query, key, value, value_gate, tables)
    tick([out], free=True)
    pu = [Gather(e["pu"][0], 0), Gather(e["pu"][1], 1)]
    tick(pu)
    e = {"mixed": mixed_b, "cot": e["cot"], "down": e["down"]}
    fence(e, done=[out] + pu)
    tick(pu)
    down = Gather(padded(e["down"]), 0)
    mixed_b = e["mixed"]
    cot_seqs = jnp.einsum("msk,mkrd->msrd", selector, e["cot"], preferred_element_type=f32)
    cot_seqs = cot_seqs.astype(bf16).reshape(members, strip, width)
    weight_out = assembled([(out, 0, 0)], member_rows, out.part.shape[1])

    held = by_place(dot_t(mixed_b, weight_out))
    e = {"came": sum_send(held, 1), "cot": cot_seqs}
    fence(e, done=pu)
    held = sum_take(held, e["came"], 1)
    tick(pu)
    e = {
        "sum": sum_far(held),
        "cot": lax.all_to_all(e["cot"], "grp", split_axis=0, concat_axis=0, tiled=True),
    }
    fence(e, done=pu)

    hidden = x + e["sum"]
    out_grad = e["cot"].reshape(own_rows, width).astype(f32) * live
    normed_mid, mid_pullback = jax.vjp(norm_rows, hidden, gain_two)
    tick(pu + [down])
    e = {"mid": pieces_far(normed_mid.astype(bf16)), "cot": out_grad.astype(bf16)}
    fence(e, done=pu + [down])
    tick([down])
    e = {"mid": rows_near(e["mid"]), "cot": pieces_far(e["cot"])}
    fence(e, rings=[down])

    middle = e["mid"]
    hid = pu[0].part.shape[1]
    weight_pu = assembled([(pu[0], 0, 0), (pu[1], 0, hid)], member_rows, 2 * hid)
    pu_pre = dot(middle, weight_pu)
    proj_pre, up_pre = pu_pre[:, :hid], pu_pre[:, hid:]
    out_grad_full = rows_near(e["cot"])

    def glu_act(proj_pre, up_pre):
        return jax.nn.gelu(proj_pre, approximate=True) * up_pre

    glu_rows, glu_pullback = jax.vjp(glu_act, proj_pre, up_pre)
    glu_b = glu_rows.astype(bf16)
    tick([down])
    ring_down = [Scatter(out_grad_full, glu_b, 0)]
    e = {"cot": out_grad_full, "glu": glu_b}
    fence(e, done=[down])
    tick([down])
    weight_down = assembled([(down, 0, 0)], member_rows, down.part.shape[1])
    proj_grad, up_grad = glu_pullback(dot(e["cot"], weight_down))
    pu_grad = jnp.concatenate([proj_grad, up_grad], axis=1).astype(bf16)
    held = by_place(dot_t(pu_grad, weight_pu))
    glu_b = e["glu"]
    e = {"came": sum_send(held, 1), "pu": pu_grad}
    fence(e)
    ring_ff = [Scatter(middle, e["pu"][:, :hid], 0), Scatter(middle, e["pu"][:, hid:], 1)]
    held = sum_take(held, e["came"], 1)
    tick(ring_ff)
    ring_ff = ring_ff + ring_down
    e = {"sum": sum_far(held), "glu": glu_b}
    fence(e)
    glu_b = e["glu"]

    hidden_grad = out_grad + mid_pullback(e["sum"])[0]
    tick(ring_ff)
    e = {"branch": pieces_far(hidden_grad.astype(bf16)), "glu": glu_b}
    fence(e, rings=ring_ff)
    tick(ring_ff)
    held = by_place(dot_t(e["glu"], weight_down))
    e = {"branch": rows_near(e["branch"]), "rows": sum_send(held, 1)}
    fence(e, rings=ring_ff)
    branch = e["branch"]

    mixed_grad = dot(branch, weight_out)
    query_grad, gate_grad, key_grad, value_grad = mixed_rows_back(
        query, key, value, value_gate, tables, weights, mixed_grad, cosine, sine
    )
    tick(ring_ff)
    held = sum_take(held, e["rows"], 1)
    ring_og = [Scatter(acts, gate_grad, 0), Scatter(branch, mixed_b, 1)]
    tick(ring_og)
    e = {
        "qk": jnp.concatenate([query_grad, key_grad], axis=1),
        "value": value_grad,
        "gate": gate_grad,
        "rows": sum_far(held),
    }
    fence(e, rings=ring_ff)
    qk_grad, value_grad, gate_grad = e["qk"], e["value"], e["gate"]
    out_rows = hidden + e["rows"]
    tick(ring_og)
    ff = [ring.whole() for ring in ring_ff]
    ring_v = Scatter(acts, value_grad, 1)
    ring_qk = Scatter(acts, qk_grad, 0)
    e = {
        "qk": qk_grad,
        "full": [ring_v.full, ring_qk.full],
        "pu": pieces_far(jnp.concatenate(ff[:2], axis=1)),
        "rows": lax.all_to_all(
            out_rows.astype(bf16).reshape(members, strip, width),
            "grp",
            split_axis=0,
            concat_axis=0,
            tiled=True,
        ),
        "down": ff[2],
    }
    fence(e, rings=ring_og)
    qk_grad, pu_far = e["qk"], e["pu"]
    ring_v.full, ring_qk.full = e["full"]
    out_seqs = e["rows"].reshape(micro, seqs, strip, width)
    out_bins = jnp.einsum("msk,msrd->mkrd", selector, out_seqs, preferred_element_type=f32)

    tick(ring_og + [ring_v, ring_qk])
    vg_grad = jnp.concatenate([value_grad, gate_grad], axis=1)
    held = by_place(dot_t(qk_grad, weight_qk) + dot_t(vg_grad, weight_vg))
    e = {
        "came": sum_send(held, 1),
        "pu": pieces_near(pu_far),
        "bins": lax.all_to_all(
            out_bins.astype(bf16), "rep", split_axis=1, concat_axis=1, tiled=True
        ),
        "down": slab_rows(e["down"][:, :hid_cols]),
    }
    fence(e, rings=ring_og)
    bin_out = e["bins"].reshape(micro, 1, block, width)
    held = sum_take(held, e["came"], 1)
    tick(ring_og + [ring_v, ring_qk])
    e = {"sum": sum_far(held), "down": e["down"], "pu": e["pu"]}
    fence(e, rings=[ring_v, ring_qk], done=ring_og)
    gate_part, out_mine = ring_og[0].whole(), slab_rows(ring_og[1].whole()[:, :val_cols])
    input_grad = hidden_grad + norm_pullback(e["sum"])[0]
    tick([ring_v, ring_qk])
    e = {
        "rows": lax.all_to_all(
            input_grad.astype(bf16).reshape(members, strip, width),
            "grp",
            split_axis=0,
            concat_axis=0,
            tiled=True,
        ),
        "gate": pieces_far(gate_part),
        "slabs": jnp.concatenate([e["down"], out_mine], axis=1),
        "pu": e["pu"],
    }
    fence(e, rings=[ring_v, ring_qk])
    token_grad = e["rows"].reshape(tokens.shape)

    tick([ring_v, ring_qk])
    proj_owned, up_owned, gain_two_owned = finished(
        e["pu"], ((0, hid_cols), (hid, hid_cols)), mlp_gain, (w_proj, w_up)
    )
    e = {
        "gate": pieces_near(e["gate"]),
        "slabs": pieces_far(e["slabs"]),
        "gain": gain_two_owned,
    }
    fence(e, done=[ring_v, ring_qk])
    gain_two_owned = e["gain"]
    gate_owned, gate_sum = finished(e["gate"], ((0, val_cols),), norm_gain, (w_gate,))
    e = {
        "slabs": pieces_near(e["slabs"]),
        "last": pieces_far(jnp.concatenate([ring_qk.whole(), ring_v.whole()], axis=1)),
        "gain": gate_sum,
    }
    fence(e)
    size = width // reps
    down_owned, out_owned = finished(e["slabs"], ((0, size), (size, size)))
    query_owned, key_owned, value_owned, rest_sum = finished(
        pieces_near(e["last"]),
        ((0, qk_cols), (qk_cols, qk_cols), (2 * qk_cols, val_cols)),
        norm_gain,
        (w_query, w_key, w_value),
    )
    gain_one_owned = (e["gain"] + rest_sum)[:, 0]
    gain_two_owned = gain_two_owned[:, 0]
    return (
        bin_out,
        token_grad,
        gain_one_owned,
        query_owned,
        key_owned,
        value_owned,
        gate_owned,
        out_owned,
        gain_two_owned,
        proj_owned,
        up_owned,
        down_owned,
    )


def solution(mesh):
    return jax.shard_map(
        body,
        mesh=mesh,
        in_specs=(
            P(None, None, "grp", "rep", None),
            P(None, "rep", "grp", None),
            P(),
            P(),
            P("grp"),
            P("grp", None),
            P("grp", None),
            P("grp", None),
            P("grp", None),
            P("grp", None),
            P("grp"),
            P("grp", None),
            P("grp", None),
            P("grp", None),
        ),
        out_specs=(
            P(None, "rep", "grp", None),
            P(None, None, "grp", "rep", None),
            P("grp"),
            P("grp", None),
            P("grp", None),
            P("grp", None),
            P("grp", None),
            P("grp", None),
            P("grp"),
            P("grp", None),
            P("grp", None),
            P("grp", None),
        ),
        check_vma=False,
    )
```

```python
import functools
import math

import jax
import jax.numpy as jnp
from jax import lax
from jax.experimental import pallas as pl
from jax.experimental.pallas import tpu as pltpu
from jax.sharding import PartitionSpec as P

HEADS = 8
KEY_DIM = 256
VAL_DIM = 432

EPS = 1e-06
GROUP_EPS = 1.0

f32 = jnp.float32
bf16 = jnp.bfloat16


def norm_rows(values, gain_vec):
    return values * lax.rsqrt(jnp.mean(values * values, axis=-1, keepdims=True) + EPS) * gain_vec


def dot(left, right):
    return jnp.dot(left, right, preferred_element_type=f32)


def dot_t(left, right):
    return lax.dot_general(left, right, (((1,), (1,)), ((), ())), preferred_element_type=f32)


def t_dot(left, right):
    return lax.dot_general(left, right, (((0,), (0,)), ((), ())), preferred_element_type=f32)


def swap(value, bit):
    count = lax.axis_size("rep")
    return lax.ppermute(value, "rep", [(i, i ^ bit) for i in range(count)])


def bits_high():
    count = lax.axis_size("rep")
    return [1 << b for b in reversed(range(count.bit_length() - 1))]


latest = {}


def fence(*states, rings=(), done=()):
    leaves, tree = jax.tree.flatten(states)
    marks = [mark for ring in rings for mark in ring.marks(2)]
    marks += [mark for ring in done for mark in ring.marks(1)]
    fenced = lax.optimization_barrier((leaves, marks))[0]
    latest["mark"] = min(fenced, key=lambda leaf: leaf.size)
    for state, new in zip(states, jax.tree.unflatten(tree, fenced)):
        state.update(new)


def pieces_far(value):
    pieces = {0: value}
    for bit in bits_high()[:-1]:
        for place in list(pieces):
            pieces[place | bit] = swap(pieces[place], bit)
    return pieces


def pieces_near(pieces):
    pieces = dict(pieces)
    for place in list(pieces):
        pieces[place | 1] = swap(pieces[place], 1)
    return [pieces[place] for place in range(len(pieces))]


def pieces_of_replicas(value):
    return pieces_near(pieces_far(value))


def rows_near(pieces):
    return jnp.concatenate(pieces_near(pieces), axis=0)


def sum_send(held, bit):
    places = [o for o in held if not o & bit]
    sent = jnp.concatenate([held[o | bit].astype(bf16) for o in places], axis=0)
    return swap(sent, bit)


def sum_take(held, came, bit):
    places = [o for o in held if not o & bit]
    rows = came.shape[0] // len(places)
    return {
        o: held[o].astype(f32) + came[i * rows : (i + 1) * rows].astype(f32)
        for i, o in enumerate(places)
    }


def by_place(partial):
    count = lax.axis_size("rep")
    rows = partial.shape[0] // count
    return {o: partial[o * rows : (o + 1) * rows] for o in range(count)}


def sum_far(held):
    for bit in reversed(bits_high()[:-1]):
        held = sum_take(held, sum_send(held, bit), bit)
    return held[0]


def own_columns(weight):
    count = lax.axis_size("rep")
    width = weight.shape[1] // count
    return lax.dynamic_slice_in_dim(weight, lax.axis_index("rep") * width, width, 1)


def ring_members():
    count = lax.axis_size("grp")
    return list(range(0, count, 2)) + list(range(count - 1, 0, -2))


def ring_place():
    count, member = lax.axis_size("grp"), lax.axis_index("grp")
    return jnp.where(member % 2 == 0, member // 2, count - (member + 1) // 2)


def ring_step(value, ahead):
    ring = ring_members()
    count = len(ring)
    return lax.ppermute(
        value, "grp", [(ring[i], ring[(i + ahead) % count]) for i in range(count)]
    )


def ring_member(ahead):
    count = lax.axis_size("grp")
    place = (ring_place() + ahead) % count
    return jnp.where(place < count // 2, 2 * place, 2 * (count - place) - 1)


def gather_members(part):
    return lax.all_gather(part, "grp", axis=0, tiled=True)


def scatter_members(full):
    return lax.psum_scatter(full, "grp", scatter_dimension=0, tiled=True)


class Ring:
    def __init__(self, wide):
        half = lax.axis_size("grp") // 2
        self.left = [half if way == wide else half - 1 for way in (0, 1)]
        self.came = [[], []]

    def rest(self):
        while max(self.left) > 0:
            self.tick(free=True)

    def marks(self, back):
        return [came[-back] for came in self.came if len(came) >= back]

    def tick(self, free=False):
        for way, ahead in enumerate((1, -1)):
            if self.left[way] > 0:
                value = self.next(way, ahead)
                if not free:
                    value = lax.optimization_barrier((value, latest["mark"]))[0]
                self.came[way].append(ring_step(value, ahead))
                self.left[way] -= 1


class Gather(Ring):
    def __init__(self, part, wide):
        super().__init__(wide)
        self.part = part

    def next(self, way, ahead):
        return self.came[way][-1] if self.came[way] else self.part

    def pieces(self):
        self.rest()
        count = lax.axis_size("grp")
        pieces = {0: self.part}
        for way, ahead in enumerate((1, -1)):
            for i, came in enumerate(self.came[way]):
                pieces[-ahead * (i + 1) % count] = came
        return [pieces[i] for i in range(count)]


class Scatter(Ring):
    def __init__(self, rows, grad, wide):
        super().__init__(wide)
        self.full = t_dot(rows, grad).astype(bf16)

    def term(self, i):
        size = self.full.shape[0] // lax.axis_size("grp")
        return lax.dynamic_slice_in_dim(self.full, ring_member(i) * size, size, 0)

    def next(self, way, ahead):
        term = self.term((ahead * self.left[way]) % lax.axis_size("grp"))
        if self.came[way]:
            term = term.astype(f32) + self.came[way][-1].astype(f32)
        return term.astype(bf16)

    def whole(self):
        self.rest()
        total = self.term(0).astype(f32)
        for came in self.came:
            total = total + came[-1].astype(f32)
        return total.astype(bf16)


def assemble_kernel(spots, order_ref, *refs):
    pieces, full_ref, sems = refs[:-2], refs[-2], refs[-1]
    copies = []
    for i, (place, member_rows, row, column) in enumerate(spots):
        rows, columns = pieces[i].shape
        start = pl.multiple_of(order_ref[place] * member_rows + row, rows)
        spot = full_ref.at[pl.ds(start, rows), pl.ds(column, columns)]
        copies.append(pltpu.make_async_copy(pieces[i], spot, sems.at[i]))
    for copy in copies:
        copy.start()
    for copy in copies:
        copy.wait()


def assembled(streams, member_rows, columns):
    members = lax.axis_size("grp")
    order = jnp.stack([ring_member(i) for i in range(members)]).astype(jnp.int32)
    pieces, spots = [], []
    for gather, row, column in streams:
        for i, piece in enumerate(gather.pieces()):
            pieces.append(piece)
            spots.append((i, member_rows, row, column))
    dtype = pieces[0].dtype
    size = members * member_rows * columns * dtype.itemsize
    return pl.pallas_call(
        functools.partial(assemble_kernel, spots),
        out_shape=jax.ShapeDtypeStruct((members * member_rows, columns), dtype),
        in_specs=[pl.BlockSpec(memory_space=pltpu.SMEM)]
        + [pl.BlockSpec(memory_space=pltpu.VMEM)] * len(pieces),
        out_specs=pl.BlockSpec(memory_space=pl.ANY),
        scratch_shapes=[pltpu.SemaphoreType.DMA((len(pieces),))],
        compiler_params=pltpu.CompilerParams(vmem_limit_bytes=size + (2 << 20)),
        cost_estimate=pl.CostEstimate(flops=0, bytes_accessed=2 * size, transcendentals=0),
    )(order, *pieces)


def finish_kernel(reps, spots, summed, rank_ref, *refs):
    count = len(spots)
    pieces, refs = refs[:reps], refs[reps:]
    if summed:
        gain_ref, refs = refs[0], refs[1:]
        weights, refs = refs[:count], refs[count:]
    outs, refs = refs[:count], refs[count:]

    def lay(rank):
        for out_ref, (column, width) in zip(outs, spots):
            for r in range(reps):
                piece = pieces[rank ^ r][:, column : column + width].astype(f32)
                out_ref[:, r * width : (r + 1) * width] = piece

    for rank in range(reps):
        pl.when(rank_ref[0] == rank)(functools.partial(lay, rank))
    if summed:
        total = 0.0
        for out_ref, weight in zip(outs, weights):
            grad = out_ref[...]
            total += jnp.sum(weight[...].astype(f32) * grad, axis=1, keepdims=True)
        refs[0][...] = total / gain_ref[...].astype(f32)


def finished(pieces, spots, gain=None, weights=()):
    reps = len(pieces)
    rows, columns = pieces[0].shape
    step = rows
    for candidate in (64, 48, 72, 32):
        if rows % candidate == 0:
            step = candidate
            break
    rank = lax.axis_index("rep").astype(jnp.int32).reshape(1)

    def blocked(width):
        return pl.BlockSpec((step, width), lambda i: (i, 0))

    operands = [rank, *pieces]
    in_specs = [pl.BlockSpec(memory_space=pltpu.SMEM)] + [blocked(columns)] * reps
    shapes = [jax.ShapeDtypeStruct((rows, reps * width), f32) for _, width in spots]
    out_specs = [blocked(reps * width) for _, width in spots]
    if gain is not None:
        operands += [gain[:, None], *weights]
        in_specs += [blocked(1)] + [blocked(weight.shape[1]) for weight in weights]
        shapes.append(jax.ShapeDtypeStruct((rows, 1), f32))
        out_specs.append(blocked(1))
    size = sum(reps * width for _, width in spots) * rows
    return pl.pallas_call(
        functools.partial(finish_kernel, reps, spots, gain is not None),
        grid=(rows // step,),
        in_specs=in_specs,
        out_specs=out_specs,
        out_shape=shapes,
        compiler_params=pltpu.CompilerParams(vmem_limit_bytes=40 << 20),
        cost_estimate=pl.CostEstimate(flops=4 * size, bytes_accessed=8 * size, transcendentals=0),
    )(*operands)


def mixed_kernel(heads, q_ref, k_ref, v_ref, gate_ref, grow_ref, shrink_ref, row_ref, column_ref,
                 mixed_ref, weights_ref):
    seen = row_ref[...] >= column_ref[...]
    if mixed_ref.shape[1] > heads * VAL_DIM:
        mixed_ref[...] = jnp.zeros_like(mixed_ref)
    for h in range(heads):
        keys, cols = slice(h * KEY_DIM, (h + 1) * KEY_DIM), slice(h * VAL_DIM, (h + 1) * VAL_DIM)
        decay = jnp.where(seen, grow_ref[:, h : h + 1] * shrink_ref[h : h + 1, :], 0.0)
        weights = (dot_t(q_ref[:, keys], k_ref[:, keys]) * decay).astype(bf16)
        weights_ref[h] = weights
        retained = dot(weights, v_ref[:, cols])
        scale = lax.rsqrt(jnp.mean(retained * retained, axis=-1, keepdims=True) + GROUP_EPS)
        gate = gate_ref[:, cols]
        mixed_ref[:, cols] = (gate * jax.nn.sigmoid(gate) * (retained * scale)).astype(bf16)


def mixed_grad_kernel(heads, q_ref, k_ref, v_ref, gate_ref, grow_ref, shrink_ref, row_ref,
                      column_ref, weights_ref, grad_ref, cos_ref, sin_ref, all_cos_ref, all_sin_ref,
                      dq_ref, dgate_ref, dk_ref, dv_ref, dk_sum, dv_sum):
    seen = row_ref[...] >= column_ref[...]
    half = KEY_DIM // 2

    def turned_back(grad, cosine, sine):
        front, back = grad[:, :half], grad[:, half:]
        return front * cosine + back * sine, back * cosine - front * sine

    @pl.when(pl.program_id(0) == 0)
    def _():
        dk_sum[...] = jnp.zeros_like(dk_sum)
        dv_sum[...] = jnp.zeros_like(dv_sum)

    if dgate_ref.shape[1] > heads * VAL_DIM:
        dgate_ref[...] = jnp.zeros_like(dgate_ref)
    for h in range(heads):
        keys, cols = slice(h * KEY_DIM, (h + 1) * KEY_DIM), slice(h * VAL_DIM, (h + 1) * VAL_DIM)
        weights, value = weights_ref[h], v_ref[:, cols]
        retained = dot(weights, value)
        scale = lax.rsqrt(jnp.mean(retained * retained, axis=-1, keepdims=True) + GROUP_EPS)
        normed = retained * scale
        gate, grad = gate_ref[:, cols], grad_ref[:, cols]
        sig = jax.nn.sigmoid(gate)
        dgate_ref[:, cols] = (grad * normed * (sig * (1.0 + gate * (1.0 - sig)))).astype(bf16)
        dnormed = grad * (gate * sig)
        slope = jnp.mean(dnormed * normed, axis=-1, keepdims=True)
        dretained = (scale * (dnormed - normed * slope)).astype(bf16)
        decay = jnp.where(seen, grow_ref[:, h : h + 1] * shrink_ref[h : h + 1, :], 0.0)
        dscores = (dot_t(dretained, value) * decay).astype(bf16)
        front, back = turned_back(dot(dscores, k_ref[:, keys]), cos_ref[...], sin_ref[...])
        dq_ref[:, h * KEY_DIM : h * KEY_DIM + half] = front.astype(bf16)
        dq_ref[:, h * KEY_DIM + half : (h + 1) * KEY_DIM] = back.astype(bf16)
        dk_sum[h] += t_dot(dscores, q_ref[:, keys])
        dv_sum[h] += t_dot(weights, dretained)

    @pl.when(pl.program_id(0) == pl.num_programs(0) - 1)
    def _():
        if dv_ref.shape[1] > heads * VAL_DIM:
            dv_ref[...] = jnp.zeros_like(dv_ref)
        for h in range(heads):
            front, back = turned_back(dk_sum[h], all_cos_ref[...], all_sin_ref[...])
            dk_ref[:, h * KEY_DIM : h * KEY_DIM + half] = front.astype(bf16)
            dk_ref[:, h * KEY_DIM + half : (h + 1) * KEY_DIM] = back.astype(bf16)
            dv_ref[:, h * VAL_DIM : (h + 1) * VAL_DIM] = dv_sum[h].astype(bf16)


def retention_specs(heads, step, rows, value_cols):
    def block(width, at=0):
        return pl.BlockSpec((step, width), lambda i: (i, at))

    def whole(height, width):
        return pl.BlockSpec((height, width), lambda i: (0, 0))

    return [
        block(heads * KEY_DIM),
        whole(rows, heads * KEY_DIM),
        whole(rows, value_cols),
        block(value_cols, 1),
        block(heads),
        whole(heads, rows),
        block(1),
        whole(1, rows),
    ], block, whole


def mixed_rows(query, key, value, value_gate, tables):
    rows, value_cols = value.shape
    heads = query.shape[1] // KEY_DIM
    step = min(rows, 256)
    specs, block, _ = retention_specs(heads, step, rows, value_cols)
    return pl.pallas_call(
        functools.partial(mixed_kernel, heads),
        grid=(rows // step,),
        in_specs=specs,
        out_specs=[
            block(value_cols),
            pl.BlockSpec((heads, step, rows), lambda i: (0, i, 0)),
        ],
        out_shape=[
            jax.ShapeDtypeStruct((rows, value_cols), bf16),
            jax.ShapeDtypeStruct((heads, rows, rows), bf16),
        ],
        compiler_params=pltpu.CompilerParams(vmem_limit_bytes=48 << 20),
        cost_estimate=pl.CostEstimate(
            flops=2 * heads * rows * rows * (KEY_DIM + VAL_DIM),
            bytes_accessed=heads * rows * rows * 2 + rows * value_cols * 8,
            transcendentals=rows * value_cols,
        ),
    )(query, key, value, value_gate, *tables)


def mixed_rows_back(query, key, value, value_gate, tables, weights, grad, cosine, sine):
    rows, value_cols = value.shape
    heads = query.shape[1] // KEY_DIM
    step = min(rows, 256)
    half = KEY_DIM // 2
    specs, block, whole = retention_specs(heads, step, rows, value_cols)
    return pl.pallas_call(
        functools.partial(mixed_grad_kernel, heads),
        grid=(rows // step,),
        in_specs=specs
        + [pl.BlockSpec((heads, step, rows), lambda i: (0, i, 0)), block(value_cols)]
        + [block(half)] * 2
        + [whole(rows, half)] * 2,
        out_specs=[
            block(heads * KEY_DIM),
            block(value_cols),
            whole(rows, heads * KEY_DIM),
            whole(rows, value_cols),
        ],
        out_shape=[
            jax.ShapeDtypeStruct((rows, heads * KEY_DIM), bf16),
            jax.ShapeDtypeStruct((rows, value_cols), bf16),
            jax.ShapeDtypeStruct((rows, heads * KEY_DIM), bf16),
            jax.ShapeDtypeStruct((rows, value_cols), bf16),
        ],
        scratch_shapes=[
            pltpu.VMEM((heads, rows, KEY_DIM), f32),
            pltpu.VMEM((heads, rows, VAL_DIM), f32),
        ],
        compiler_params=pltpu.CompilerParams(vmem_limit_bytes=56 << 20),
        cost_estimate=pl.CostEstimate(
            flops=2 * heads * rows * rows * (2 * KEY_DIM + 3 * VAL_DIM),
            bytes_accessed=heads * rows * rows * 2 + rows * value_cols * 16,
            transcendentals=rows * value_cols,
        ),
    )(query, key, value, value_gate, *tables, weights, grad, cosine, sine, cosine, sine)


def slab_routes():
    reps, members = lax.axis_size("rep"), lax.axis_size("grp")
    per = members // reps
    return [
        [
            (s * members + m, (m // per) * members + per * s + (m % per + turn) % per)
            for s in range(reps)
            for m in range(members)
        ]
        for turn in range(per)
    ]


def selected(choices, which):
    result = choices[0]
    for s in range(1, len(choices)):
        result = jnp.where(which == s, choices[s], result)
    return result


def slab_parts(weight):
    reps, members = lax.axis_size("rep"), lax.axis_size("grp")
    rank, member = lax.axis_index("rep"), lax.axis_index("grp")
    per = members // reps
    size = weight.shape[1] // members
    blocks = [per * rank + (member % per + turn) % per for turn in range(per)]
    return [lax.dynamic_slice_in_dim(weight, block * size, size, 1).T for block in blocks]


def slab_piece(parts):
    reps, members = lax.axis_size("rep"), lax.axis_size("grp")
    member = lax.axis_index("grp")
    per = members // reps
    came = [
        lax.ppermute(sent, ("rep", "grp"), route) for sent, route in zip(parts, slab_routes())
    ]
    return jnp.concatenate(
        [selected([came[(e - a) % per] for e in range(per)], member % per) for a in range(per)],
        axis=1,
    )


def slab_rows(owned):
    reps, members = lax.axis_size("rep"), lax.axis_size("grp")
    member = lax.axis_index("grp")
    per = members // reps
    rows = owned.shape[1] // per
    came = []
    for turn, route in enumerate(slab_routes()):
        owner = (member % per - turn + per) % per
        sent = lax.dynamic_slice_in_dim(owned, owner * rows, rows, 1)
        came.append(lax.ppermute(sent, ("rep", "grp"), [(b, a) for a, b in route]))
    mine = jnp.concatenate(
        [
            selected([came[(k - e) % per] for e in range(per)], member % per).T
            for k in range(per)
        ],
        axis=1,
    )
    return mine


def padded(value):
    gap = -value.shape[1] % 128
    return jnp.pad(value, ((0, 0), (0, gap))) if gap else value


def body(
    tokens,
    cotangent,
    seq_lengths,
    bin_order,
    norm_gain,
    w_query,
    w_key,
    w_value,
    w_gate,
    w_out,
    mlp_gain,
    w_proj,
    w_up,
    w_down,
):
    reps, members = lax.axis_size("rep"), lax.axis_size("grp")
    rank, member = lax.axis_index("rep"), lax.axis_index("grp")
    micro, seqs, _, strip, width = tokens.shape
    own_rows = members * strip
    block = reps * strip
    heads = HEADS // reps
    qk_cols = heads * KEY_DIM
    val_cols = heads * VAL_DIM
    hid_cols = w_proj.shape[1] // reps
    member_rows = width // members

    strip_pos = (
        jnp.arange(members, dtype=jnp.int32)[:, None] * block
        + jnp.arange(strip, dtype=jnp.int32)[None, :]
    ).reshape(own_rows)
    positions = jnp.concatenate([strip_pos + strip * (rank ^ o) for o in range(reps)])
    live_len = lax.dynamic_index_in_dim(seq_lengths.reshape(-1), member, 0, False)
    live = (positions[:own_rows] < live_len).astype(f32)[:, None]
    selector = (
        bin_order[:, :, None] == jnp.arange(seqs, dtype=jnp.int32)[None, None, :]
    ).astype(bf16)

    qk = Gather(jnp.concatenate([own_columns(w_query), own_columns(w_key)], axis=1), 0)
    vg = Gather(
        jnp.concatenate([padded(own_columns(w_value)), padded(own_columns(w_gate))], axis=1), 1
    )

    def tick(rings, free=False):
        for ring in rings:
            ring.tick(free)

    frequency = jnp.exp(
        -jnp.arange(KEY_DIM // 2, dtype=f32) * (2.0 / KEY_DIM) * math.log(10000.0)
    )
    angles = positions.astype(f32)[:, None] * frequency[None, :]
    log_gamma = jnp.log(1.0 - jnp.exp2(-5.0 - (rank * heads + jnp.arange(heads)).astype(f32)))
    spans = positions.astype(f32)[None, :] * log_gamma[:, None]
    t = {
        "cos": jnp.cos(angles),
        "sin": jnp.sin(angles),
        "grow": jnp.exp(spans).T,
        "shrink": jnp.exp(-spans),
    }

    for _ in range(members // 2):
        tick([qk, vg], free=True)
    e = {
        "rows": lax.all_to_all(
            tokens.reshape(members, strip, width), "grp", split_axis=0, concat_axis=0, tiled=True
        ),
        "out": slab_parts(w_out),
        "down": slab_parts(w_down),
        "pu": [padded(own_columns(w_proj)), padded(own_columns(w_up))],
        "gains": lax.all_to_all(
            jnp.broadcast_to(jnp.stack([norm_gain, mlp_gain]), (members, 2, member_rows)),
            "grp",
            split_axis=0,
            concat_axis=0,
            tiled=True,
        ),
    }
    fence(e, t)
    cosine, sine = t["cos"], t["sin"]
    def turn(pre):
        half = KEY_DIM // 2
        front, back = pre[:, :half], pre[:, half:]
        return jnp.concatenate(
            [front * cosine - back * sine, back * cosine + front * sine], axis=1
        )

    tables = (t["grow"], t["shrink"], positions[:, None], positions[None, :])

    x = e["rows"].reshape(own_rows, width).astype(f32)
    gains = e.pop("gains").transpose(1, 0, 2).reshape(2, width).astype(f32)
    gain_one, gain_two = gains[0], gains[1]
    normed, norm_pullback = jax.vjp(norm_rows, x, gain_one)
    e["acts"] = normed.astype(bf16)
    e["cot"] = lax.all_to_all(
        cotangent.reshape(micro, reps, strip, width), "rep", split_axis=1, concat_axis=1, tiled=True
    )
    del e["rows"]
    fence(e)
    e["acts"] = pieces_far(e["acts"])
    fence(e)
    e["acts"] = rows_near(e["acts"])
    e["out"] = slab_piece(e["out"])
    fence(e)
    out = Gather(padded(e.pop("out")), 0)

    acts = e["acts"]
    weight_qk = assembled([(qk, 0, 0)], member_rows, 2 * qk_cols)
    tick([out])
    pre = dot(acts, weight_qk)
    def turned(at):
        parts = [
            turn(pre[:, at + h * KEY_DIM : at + (h + 1) * KEY_DIM]).astype(bf16)
            for h in range(heads)
        ]
        return jnp.concatenate(parts, axis=1)

    query, key = turned(0), turned(qk_cols)
    e = {
        "query": query,
        "key": key,
        "cot": e["cot"],
        "down": e["down"],
        "pu": e["pu"],
        "acts": acts,
    }
    fence(e, done=[vg])
    query, key, acts = e["query"], e["key"], e["acts"]
    weight_vg = assembled([(vg, 0, 0)], member_rows, vg.part.shape[1])
    tick([out])
    gate_at = vg.part.shape[1] // 2
    value_gate = dot(acts, weight_vg)
    e = {
        "cot": e["cot"],
        "down": slab_piece(e["down"]),
        "pu": e["pu"],
        "value": value_gate[:, :gate_at].astype(bf16),
    }
    fence(e, done=[out])
    value = e["value"]
    tick([out])

    mixed_b, weights = mixed_rows(query, key, value, value_gate, tables)
    tick([out], free=True)
    pu = [Gather(e["pu"][0], 0), Gather(e["pu"][1], 1)]
    tick(pu)
    e = {"mixed": mixed_b, "cot": e["cot"], "down": e["down"]}
    fence(e, done=[out] + pu)
    tick(pu)
    down = Gather(padded(e["down"]), 0)
    mixed_b = e["mixed"]
    cot_seqs = jnp.einsum("msk,mkrd->msrd", selector, e["cot"], preferred_element_type=f32)
    cot_seqs = cot_seqs.astype(bf16).reshape(members, strip, width)
    weight_out = assembled([(out, 0, 0)], member_rows, out.part.shape[1])

    held = by_place(dot_t(mixed_b, weight_out))
    e = {"came": sum_send(held, 1), "cot": cot_seqs}
    fence(e, done=pu)
    held = sum_take(held, e["came"], 1)
    tick(pu)
    e = {
        "sum": sum_far(held),
        "cot": lax.all_to_all(e["cot"], "grp", split_axis=0, concat_axis=0, tiled=True),
    }
    fence(e, done=pu)

    hidden = x + e["sum"]
    out_grad = e["cot"].reshape(own_rows, width).astype(f32) * live
    normed_mid, mid_pullback = jax.vjp(norm_rows, hidden, gain_two)
    tick(pu + [down])
    e = {"mid": pieces_far(normed_mid.astype(bf16)), "cot": out_grad.astype(bf16)}
    fence(e, done=pu + [down])
    tick([down])
    e = {"mid": rows_near(e["mid"]), "cot": pieces_far(e["cot"])}
    fence(e, rings=[down])

    middle = e["mid"]
    hid = pu[0].part.shape[1]
    weight_pu = assembled([(pu[0], 0, 0), (pu[1], 0, hid)], member_rows, 2 * hid)
    pu_pre = dot(middle, weight_pu)
    proj_pre, up_pre = pu_pre[:, :hid], pu_pre[:, hid:]
    out_grad_full = rows_near(e["cot"])

    def glu_act(proj_pre, up_pre):
        return jax.nn.gelu(proj_pre, approximate=True) * up_pre

    glu_rows, glu_pullback = jax.vjp(glu_act, proj_pre, up_pre)
    glu_b = glu_rows.astype(bf16)
    tick([down])
    ring_down = [Scatter(out_grad_full, glu_b, 0)]
    e = {"cot": out_grad_full, "glu": glu_b}
    fence(e, done=[down])
    tick([down])
    weight_down = assembled([(down, 0, 0)], member_rows, down.part.shape[1])
    proj_grad, up_grad = glu_pullback(dot(e["cot"], weight_down))
    pu_grad = jnp.concatenate([proj_grad, up_grad], axis=1).astype(bf16)
    held = by_place(dot_t(pu_grad, weight_pu))
    glu_b = e["glu"]
    e = {"came": sum_send(held, 1), "pu": pu_grad}
    fence(e)
    ring_ff = [Scatter(middle, e["pu"][:, :hid], 0), Scatter(middle, e["pu"][:, hid:], 1)]
    held = sum_take(held, e["came"], 1)
    tick(ring_ff)
    ring_ff = ring_ff + ring_down
    e = {"sum": sum_far(held), "glu": glu_b}
    fence(e)
    glu_b = e["glu"]

    hidden_grad = out_grad + mid_pullback(e["sum"])[0]
    tick(ring_ff)
    e = {"branch": pieces_far(hidden_grad.astype(bf16)), "glu": glu_b}
    fence(e, rings=ring_ff)
    tick(ring_ff)
    held = by_place(dot_t(e["glu"], weight_down))
    e = {"branch": rows_near(e["branch"]), "rows": sum_send(held, 1)}
    fence(e, rings=ring_ff)
    branch = e["branch"]

    mixed_grad = dot(branch, weight_out)
    query_grad, gate_grad, key_grad, value_grad = mixed_rows_back(
        query, key, value, value_gate, tables, weights, mixed_grad, cosine, sine
    )
    tick(ring_ff)
    held = sum_take(held, e["rows"], 1)
    ring_og = [Scatter(acts, gate_grad, 0), Scatter(branch, mixed_b, 1)]
    tick(ring_og)
    e = {
        "qk": jnp.concatenate([query_grad, key_grad], axis=1),
        "value": value_grad,
        "gate": gate_grad,
        "rows": sum_far(held),
    }
    fence(e, rings=ring_ff)
    qk_grad, value_grad, gate_grad = e["qk"], e["value"], e["gate"]
    out_rows = hidden + e["rows"]
    tick(ring_og)
    ff = [ring.whole() for ring in ring_ff]
    ring_v = Scatter(acts, value_grad, 1)
    tick([ring_v])
    ring_qk = Scatter(acts, qk_grad, 0)
    e = {
        "qk": qk_grad,
        "full": ring_qk.full,
        "pu": pieces_far(jnp.concatenate(ff[:2], axis=1)),
        "rows": lax.all_to_all(
            out_rows.astype(bf16).reshape(members, strip, width),
            "grp",
            split_axis=0,
            concat_axis=0,
            tiled=True,
        ),
        "down": ff[2],
    }
    fence(e, rings=ring_og)
    qk_grad, pu_far = e["qk"], e["pu"]
    ring_qk.full = e["full"]
    out_seqs = e["rows"].reshape(micro, seqs, strip, width)
    out_bins = jnp.einsum("msk,msrd->mkrd", selector, out_seqs, preferred_element_type=f32)

    tick(ring_og + [ring_v, ring_qk])
    vg_grad = jnp.concatenate([value_grad, gate_grad], axis=1)
    held = by_place(dot_t(qk_grad, weight_qk) + dot_t(vg_grad, weight_vg))
    e = {
        "came": sum_send(held, 1),
        "pu": pieces_near(pu_far),
        "bins": lax.all_to_all(
            out_bins.astype(bf16), "rep", split_axis=1, concat_axis=1, tiled=True
        ),
        "down": slab_rows(e["down"][:, :hid_cols]),
    }
    fence(e, rings=ring_og)
    bin_out = e["bins"].reshape(micro, 1, block, width)
    held = sum_take(held, e["came"], 1)
    tick(ring_og + [ring_v, ring_qk])
    e = {"sum": sum_far(held), "down": e["down"], "pu": e["pu"]}
    fence(e, rings=[ring_v, ring_qk], done=ring_og)
    gate_part, out_mine = ring_og[0].whole(), slab_rows(ring_og[1].whole()[:, :val_cols])
    input_grad = hidden_grad + norm_pullback(e["sum"])[0]
    tick([ring_v, ring_qk])
    e = {
        "rows": input_grad.astype(bf16).reshape(members, strip, width),
        "gate": pieces_far(gate_part),
        "slabs": jnp.concatenate([e["down"], out_mine], axis=1),
        "pu": e["pu"],
    }
    fence(e, rings=[ring_v, ring_qk])
    rows_out = e["rows"]

    tick([ring_qk])
    proj_owned, up_owned, gain_two_owned = finished(
        e["pu"], ((0, hid_cols), (hid, hid_cols)), mlp_gain, (w_proj, w_up)
    )
    e = {
        "gate": pieces_near(e["gate"]),
        "slabs": pieces_far(e["slabs"]),
        "value": pieces_far(ring_v.whole()),
        "rows": rows_out,
        "gain": gain_two_owned,
    }
    fence(e, done=[ring_qk])
    gain_two_owned = e["gain"]
    gate_owned, gate_sum = finished(e["gate"], ((0, val_cols),), norm_gain, (w_gate,))
    e = {
        "slabs": pieces_near(e["slabs"]),
        "value": pieces_near(e["value"]),
        "last": pieces_far(ring_qk.whole()),
        "rows": lax.all_to_all(e["rows"], "grp", split_axis=0, concat_axis=0, tiled=True),
        "gain": gate_sum,
    }
    fence(e)
    token_grad = e["rows"].reshape(tokens.shape)
    size = width // reps
    down_owned, out_owned = finished(e["slabs"], ((0, size), (size, size)))
    value_owned, value_sum = finished(e["value"], ((0, val_cols),), norm_gain, (w_value,))
    query_owned, key_owned, rest_sum = finished(
        pieces_near(e["last"]),
        ((0, qk_cols), (qk_cols, qk_cols)),
        norm_gain,
        (w_query, w_key),
    )
    gain_one_owned = (e["gain"] + value_sum + rest_sum)[:, 0]
    gain_two_owned = gain_two_owned[:, 0]
    return (
        bin_out,
        token_grad,
        gain_one_owned,
        query_owned,
        key_owned,
        value_owned,
        gate_owned,
        out_owned,
        gain_two_owned,
        proj_owned,
        up_owned,
        down_owned,
    )


def solution(mesh):
    return jax.shard_map(
        body,
        mesh=mesh,
        in_specs=(
            P(None, None, "grp", "rep", None),
            P(None, "rep", "grp", None),
            P(),
            P(),
            P("grp"),
            P("grp", None),
            P("grp", None),
            P("grp", None),
            P("grp", None),
            P("grp", None),
            P("grp"),
            P("grp", None),
            P("grp", None),
            P("grp", None),
        ),
        out_specs=(
            P(None, "rep", "grp", None),
            P(None, None, "grp", "rep", None),
            P("grp"),
            P("grp", None),
            P("grp", None),
            P("grp", None),
            P("grp", None),
            P("grp", None),
            P("grp"),
            P("grp", None),
            P("grp", None),
            P("grp", None),
        ),
        check_vma=False,
    )
```
